32 devices in a mesh: segment: 4 (over x, core), dp: 4 (over z), seq: 2 (over y).
Axes of the slice: x: 2, y: 2, z: 4, core: 2. Of those that a mesh axis runs over, the one named last changes fastest.
Arguments:
- query_in: bfloat16 [16, 256, 1536], P(('segment', 'dp'), 'seq'), may hold values from -6 to 6
- key_in: bfloat16 [16, 256, 1536], P(('segment', 'dp'), 'seq'), may hold values from -6 to 6
- value_in: bfloat16 [16, 256, 1536], P(('segment', 'dp'), 'seq'), may hold values from -6 to 6
- latent_now: bfloat16 [16, 256, 1536], P(('segment', 'dp'), 'seq'), may hold values from -6 to 6
- latent_next: bfloat16 [16, 256, 1536], P(('segment', 'dp'), 'seq'), may hold values from -6 to 6
- norm_gains: float32 [2, 128], replicated, may hold values from 0.1 to 1.9
- rewards: float32 [16], replicated, may hold values from -2 to 2
- step_index: int32 [16], replicated, may hold values from 0 to 15
- token_count: int32 [16], replicated, may hold values from 64 to 256, as said below
Outputs:
- grad_query: bfloat16 [16, 256, 1536], P(('segment', 'dp'), None, 'seq')
- grad_key: bfloat16 [16, 256, 1536], P(('segment', 'dp'), None, 'seq')
- grad_value: bfloat16 [16, 256, 1536], P(('segment', 'dp'), None, 'seq')
- gain_grads: float32 [2, 128], replicated
The draws below stay inside these ranges and needn't reach their ends.
Inputs may be any that keep to these rules, and one draw needn't show every extreme that they name: `token_count`: valid tokens of each video; some video has exactly 256.
All inputs are finite; a program needn't handle non-finite values.
Results may differ from the reference program's by a relative error of at most 0.018.
Values may be sent and summed in bfloat16 or wider, within the bound.
A program may use at most 64 MiB of HBM per device.

```python
import jax
import jax.numpy as jnp
from jax import lax

HEADS = 12
HEAD = 128
D = 1536
SEQ = 256
STEPS = 16
GROUP = 16
VIDEOS = 16
GROUPS = 1
N_DP = 4


def draw_rewards(key, part):
    scale_key = jax.random.fold_in(key, 11)
    base_key = jax.random.fold_in(key, 12)
    scales = jnp.exp(jax.random.uniform(scale_key, (GROUPS,), jnp.float32, jnp.log(0.05), jnp.log(2.0)))
    member = jnp.arange(VIDEOS) // GROUP
    base = jax.random.uniform(base_key, (VIDEOS,), jnp.float32, -1.0, 1.0)
    return base * scales[member]


def draw_token_count(key, part):
    count_key = jax.random.fold_in(key, 21)
    full_key = jax.random.fold_in(key, 22)
    counts = jax.random.randint(count_key, (VIDEOS,), SEQ // 4, SEQ + 1)
    full = jax.random.randint(full_key, (), 0, VIDEOS)
    return jnp.where(jnp.arange(VIDEOS) == full, SEQ, counts).astype(jnp.int32)


def touch_ends(values, own_key, smallest, top_value):
    longest = values.shape.index(max(values.shape))
    spots = []
    for shift in (0, 1):
        where = [jax.random.randint(jax.random.fold_in(own_key, axis), (), 0, length) for axis, length in enumerate(values.shape)]
        where[longest] = (where[longest] + shift) % values.shape[longest]
        spots.append(tuple(where))
    return values.at[spots[0]].set(smallest).at[spots[1]].set(top_value)


def level_of(stream_key, dims, shards, smallest, top_value):
    level = 1.0
    for axis_at, shards_of in shards:
        heights = jax.random.uniform(jax.random.fold_in(jax.random.fold_in(stream_key, 6), axis_at), (shards_of,), jnp.float32, smallest / len(shards), top_value / len(shards))
        level = level * jnp.repeat(jnp.exp(heights), dims[axis_at] // shards_of).reshape((-1,) + (1,) * (len(dims) - 1 - axis_at))
    return level


def normal_values(stream_key, dims, deviation, most, pieces=(), dtype=jnp.bfloat16):
    factor_of = level_of(stream_key, dims, pieces, -0.22, 0.18) if pieces else 1.0
    array = jax.random.normal(stream_key, dims, jnp.float32) * deviation * factor_of
    return jnp.minimum(jnp.maximum(array, -most), most).astype(dtype)


def setup_inputs(seed: int = 0) -> dict:
    key_of = jax.random.split(jax.random.key(seed), 10)
    return {
        "query_in": normal_values(key_of[0], (VIDEOS, SEQ, D), 1.0, 6.0, ((0, 16), (1, 2))),
        "key_in": normal_values(key_of[1], (VIDEOS, SEQ, D), 1.0, 6.0, ((0, 16), (1, 2))),
        "value_in": normal_values(key_of[2], (VIDEOS, SEQ, D), 1.0, 6.0, ((0, 16), (1, 2))),
        "latent_now": normal_values(key_of[3], (VIDEOS, SEQ, D), 1.0, 6.0, ((0, 16), (1, 2))),
        "latent_next": normal_values(key_of[4], (VIDEOS, SEQ, D), 1.0, 6.0, ((0, 16), (1, 2))),
        "norm_gains": jnp.clip(1.0 + 0.18 * jax.random.normal(key_of[5], (2, HEAD), jnp.float32), 0.1, 1.9),
        "rewards": draw_rewards(jax.random.fold_in(key_of[9], 71), 0),
        "step_index": touch_ends(jax.random.randint(key_of[7], (VIDEOS,), 0, STEPS), jax.random.fold_in(key_of[7], 1), 0, STEPS - 1).astype(jnp.int32),
        "token_count": draw_token_count(jax.random.fold_in(key_of[9], 71), 0),
    }


def head_norm(values, gain):
    wide = values.astype(jnp.float32)
    scaled = wide * lax.rsqrt(lax.optimization_barrier(jnp.mean(wide * wide, axis=-1, keepdims=True)) + 1e-06)
    return (scaled * gain).astype(jnp.bfloat16)

def head_grads(query, keys, values, now_rows, next_rows, gains, advantage, delta, count):
    length = query.shape[0]
    keep = jnp.arange(length) < count

    def forward(q_in, k_in, v_in, gains_in):
        q_rows = head_norm(q_in, gains_in[0])
        k_rows = head_norm(k_in, gains_in[1])
        scores = jnp.dot(q_rows, k_rows.T, preferred_element_type=jnp.float32) / jnp.sqrt(jnp.float32(q_in.shape[1]))
        scores = jnp.where(keep[None, :], scores, jnp.float32(-1e+30))
        weights = jax.nn.softmax(scores, axis=-1).astype(jnp.bfloat16)
        return jnp.dot(weights, v_in, preferred_element_type=jnp.float32)
    velocity, pull = jax.vjp(forward, query, keys, values, gains)
    mean_next = now_rows.astype(jnp.float32) - delta * velocity
    cotangent = jnp.where(keep[:, None], advantage * (next_rows.astype(jnp.float32) - mean_next), jnp.float32(0.0))
    return pull(cotangent)

def group_advantage(rewards):
    total = rewards.shape[0]
    member = (jnp.arange(total)[:, None] // GROUP == jnp.arange(total // GROUP)[None, :]).astype(jnp.float32)
    means = jnp.dot(rewards, member) / GROUP
    mean_rows = jnp.dot(member, means)
    spreads = jnp.sqrt(jnp.dot((rewards - mean_rows) ** 2, member) / GROUP)
    return (rewards - mean_rows) / jnp.maximum(jnp.dot(member, spreads), jnp.float32(0.25))

def step_sigma(index):
    level = 1.0 - index.astype(jnp.float32) / STEPS
    return 7.0 * level / (1.0 + 6.0 * level)

def reference(query_in, key_in, value_in, latent_now, latent_next, norm_gains, rewards, step_index, token_count):
    advantage = jnp.roll(group_advantage(rewards), N_DP, axis=0)
    delta = jnp.roll(step_sigma(step_index) - step_sigma(step_index + 1), N_DP, axis=0)
    counts = jnp.roll(token_count, N_DP, axis=0)
    arrays = tuple((jnp.roll(a, N_DP, axis=0).reshape(VIDEOS, SEQ, HEADS, HEAD) for a in (query_in, key_in, value_in, latent_now, latent_next)))

    def one_video(items):
        q_all, k_all, v_all, now_all, next_all, adv, dlt, cnt = items
        moved = tuple((jnp.moveaxis(a, 1, 0) for a in (q_all, k_all, v_all, now_all, next_all)))
        grads = jax.vmap(lambda a, b, c, d, e: head_grads(a, b, c, d, e, norm_gains, adv, dlt, cnt))(*moved)
        return (jnp.moveaxis(grads[0], 0, 1), jnp.moveaxis(grads[1], 0, 1), jnp.moveaxis(grads[2], 0, 1), lax.optimization_barrier(jnp.sum(grads[3], axis=0)))
    dq, dk, dv, dg = lax.map(one_video, arrays + (advantage, delta, counts))
    gain_grads = lax.optimization_barrier(jnp.sum(dg, axis=0)) / VIDEOS
    return (dq.reshape(VIDEOS, SEQ, D).astype(jnp.bfloat16), dk.reshape(VIDEOS, SEQ, D).astype(jnp.bfloat16), dv.reshape(VIDEOS, SEQ, D).astype(jnp.bfloat16), gain_grads)
```

```python
import functools

import jax
import jax.numpy as jnp
from jax import lax
from jax.experimental import pallas as pl
from jax.experimental.pallas import tpu as pltpu
from jax.sharding import PartitionSpec as P

HEAD = 128
STEPS = 16
GROUP = 16
AHEAD = 3
MESH = pl.DeviceIdType.MESH
F32 = jnp.float32
BF16 = jnp.bfloat16


def dot(a, b, da, db):
    return lax.dot_general(a, b, (((da,), (db,)), ((), ())), preferred_element_type=F32)


def unit_rows(x):
    wide = x.astype(F32)
    r = lax.rsqrt(jnp.mean(wide * wide, axis=-1, keepdims=True) + 1e-06)
    return wide * r, r


def unit_rows_back(grad, unit, r, gain):
    inner = grad * gain
    mean = jnp.mean(inner * unit, axis=-1, keepdims=True)
    return r * (inner - unit * mean), jnp.sum(grad * unit, axis=0, keepdims=True)


def head_grads(q_in, k_in, v, diff, gains, advantage, delta, count):
    length = q_in.shape[0]
    scale = HEAD ** -0.5
    index = lax.broadcasted_iota(jnp.int32, (length, 1), 0)
    bias = jnp.where(index < count, F32(0.0), F32(-1e30))
    row_scale = jnp.where(index < count, advantage, F32(0.0))
    q_unit, q_r = unit_rows(q_in)
    k_unit, k_r = unit_rows(k_in)
    q = (q_unit * gains[0:1]).astype(BF16)
    k = (k_unit * gains[1:2]).astype(BF16)
    raw = jnp.exp(dot(k, q, 1, 1) * scale + bias)
    soft = raw * (1.0 / jnp.sum(raw, axis=0, keepdims=True))
    weights = soft.astype(BF16)
    velocity = dot(weights, v, 0, 0)
    cotangent = (row_scale * (diff.astype(F32) + delta * velocity)).astype(BF16)
    dv = dot(weights, cotangent, 1, 0)
    dw = dot(v, cotangent, 1, 1)
    mixed = soft * dw
    ds = (mixed - soft * jnp.sum(mixed, axis=0, keepdims=True)).astype(BF16)
    dk, dg_k = unit_rows_back(dot(ds, q, 1, 0) * scale, k_unit, k_r, gains[1:2])
    dq, dg_q = unit_rows_back(dot(ds, k, 0, 0) * scale, q_unit, q_r, gains[0:1])
    return dq.astype(BF16), dk.astype(BF16), dv.astype(BF16), dg_q, dg_k


def sigma(index):
    level = 1.0 - index.astype(F32) / STEPS
    return 7.0 * level / (1.0 + 6.0 * level)


def kernel(
    sizes,
    q_ref, k_ref, v_ref, now_ref, next_ref, gains_ref, reward_ref, step_ref, count_ref,
    oq_ref, ok_ref, ov_ref, og_ref,
    qb, kb, vb, db, lat, diff, gq, gk, gv, sum1, sum2,
    lat_sem, own_sem, send_sem, recv_sem, out_send, out_recv, s1_send, s1_recv, s2_send, s2_recv,
):
    segments, replicas, shards = sizes
    seg, dp, me = (lax.axis_index(name) for name in ("segment", "dp", "seq"))
    rows, width = q_ref.shape[1], qb.shape[1]
    heads = width // HEAD

    loads = [
        pltpu.make_async_copy(ref.at[0], lat.at[i], lat_sem.at[i])
        for i, ref in enumerate((now_ref, next_ref))
    ]
    for copy in loads:
        copy.start()

    sources = (q_ref.at[0], k_ref.at[0], v_ref.at[0], diff)
    targets = (qb, kb, vb, db)
    my_rows = pl.ds(pl.multiple_of(me * rows, rows), rows)
    own_columns = pl.ds(pl.multiple_of(me * width, width), width)
    own = [
        pltpu.make_async_copy(sources[i].at[:, own_columns], targets[i].at[my_rows, :], own_sem.at[i])
        for i in range(4)
    ]
    for copy in own[:3]:
        copy.start()

    group1 = [
        (lax.rem(seg + a, segments), dp, lax.rem(me + b, shards))
        for a in range(segments)
        for b in range(shards)
        if a or b
    ]
    group2 = [(seg, lax.rem(dp + a, replicas), me) for a in range(1, replicas)]
    barrier = pltpu.get_barrier_semaphore()
    for device in group1 + group2:
        pl.semaphore_signal(barrier, inc=1, device_id=device, device_id_type=MESH)
    pl.semaphore_wait(barrier, len(group1) + len(group2))

    def part(array, head, step):
        other = lax.rem(me + step, shards)
        columns = pl.ds(pl.multiple_of(other * width + head * HEAD, HEAD), HEAD)
        return pltpu.make_async_remote_copy(
            src_ref=sources[array].at[:, columns],
            dst_ref=targets[array].at[my_rows, pl.ds(head * HEAD, HEAD)],
            send_sem=send_sem.at[array, head, step - 1],
            recv_sem=recv_sem.at[array, head, step - 1],
            device_id=(seg, dp, other),
            device_id_type=MESH,
        )

    parts = [
        [[part(i, h, s) for s in range(1, shards)] for i in range(4)] for h in range(heads)
    ]

    def send(head, arrays):
        for i in arrays:
            for copy in parts[head][i]:
                copy.start()

    ahead = min(AHEAD, heads)
    send(0, (0, 1, 2))
    for copy in loads:
        copy.wait()
    full = diff.shape[1]
    for c in range(0, full, 256):
        cols = slice(c, c + 256)
        diff[:, cols] = (lat[1, :, cols].astype(F32) - lat[0, :, cols].astype(F32)).astype(BF16)
    send(0, (3,))
    for h in range(1, ahead):
        send(h, (0, 1, 2, 3))
    own[3].start()

    video = seg * replicas + dp
    first = video // GROUP * GROUP
    one = (1, 1)
    rewards = [reward_ref[first + i] for i in range(GROUP)]
    mean = sum(rewards[1:], rewards[0]) * F32(1.0 / GROUP)
    spread = sum((r - mean) * (r - mean) for r in rewards) * F32(1.0 / GROUP)
    spread = jnp.sqrt(jnp.full(one, spread, F32))
    advantage = jnp.full(one, reward_ref[video] - mean, F32) / jnp.maximum(spread, F32(0.25))
    step = jnp.full(one, step_ref[video], jnp.int32)
    delta = sigma(step) - sigma(step + 1)
    count = count_ref[video]
    gains = gains_ref[...]

    for copy in own:
        copy.wait()

    next_device = (lax.rem(seg + 1, segments), dp, me)
    outs = []
    dg_q = jnp.zeros((1, HEAD), F32)
    dg_k = jnp.zeros((1, HEAD), F32)
    for h in range(heads):
        for i in range(4):
            for copy in parts[h][i]:
                copy.wait_recv()
        if h + ahead < heads:
            send(h + ahead, (0, 1, 2, 3))
        cols = slice(h * HEAD, (h + 1) * HEAD)
        dq, dk, dv, a, b = head_grads(
            qb[:, cols], kb[:, cols], vb[:, cols], db[:, cols], gains, advantage, delta, count
        )
        dg_q, dg_k = dg_q + a, dg_k + b
        gq[:, cols], gk[:, cols], gv[:, cols] = dq, dk, dv
        for i, (src, dst) in enumerate(((gq, oq_ref), (gk, ok_ref), (gv, ov_ref))):
            copy = pltpu.make_async_remote_copy(
                src_ref=src.at[:, cols],
                dst_ref=dst.at[0, :, cols],
                send_sem=out_send.at[i, h],
                recv_sem=out_recv.at[i, h],
                device_id=next_device,
                device_id_type=MESH,
            )
            copy.start()
            outs.append(copy)

    def spread_sum(slots, mine, value, group, sent, received):
        slots[mine] = value
        copies = [
            pltpu.make_async_remote_copy(
                src_ref=slots.at[mine],
                dst_ref=slots.at[mine],
                send_sem=sent.at[i],
                recv_sem=received.at[i],
                device_id=device,
                device_id_type=MESH,
            )
            for i, device in enumerate(group)
        ]
        for copy in copies:
            copy.start()
        for copy in copies:
            copy.wait_recv()
        total = slots[0]
        for i in range(1, len(group) + 1):
            total = total + slots[i]
        return total, copies

    share = jnp.concatenate([dg_q, dg_k, jnp.zeros((6, HEAD), F32)], axis=0)
    total, copies1 = spread_sum(sum1, seg * shards + me, share, group1, s1_send, s1_recv)
    total, copies2 = spread_sum(sum2, dp, total, group2, s2_send, s2_recv)
    og_ref[...] = total[0:2] * F32(1.0 / (segments * replicas))

    for copy in outs:
        copy.wait()
    for copy in copies1 + copies2:
        copy.wait_send()
    for head in parts:
        for array in head:
            for copy in array:
                copy.wait_send()


def body(sizes, query_in, key_in, value_in, latent_now, latent_next, gains, rewards, steps, counts):
    segments, replicas, shards = sizes
    _, rows, full = query_in.shape
    length, width = rows * shards, full // shards
    heads = width // HEAD
    any_space = pl.BlockSpec(memory_space=pltpu.HBM)
    vmem = pl.BlockSpec(memory_space=pltpu.VMEM)
    smem = pl.BlockSpec(memory_space=pltpu.SMEM)
    grad = jax.ShapeDtypeStruct((1, length, width), BF16)
    near, far = segments * shards, replicas
    dma = pltpu.SemaphoreType.DMA
    return pl.pallas_call(
        functools.partial(kernel, sizes),
        out_shape=(grad, grad, grad, jax.ShapeDtypeStruct((2, HEAD), F32)),
        in_specs=[any_space] * 5 + [vmem] + [smem] * 3,
        out_specs=(any_space, any_space, any_space, vmem),
        scratch_shapes=[pltpu.VMEM((length, width), BF16)] * 4
        + [pltpu.VMEM((2, rows, full), BF16), pltpu.VMEM((rows, full), BF16)]
        + [pltpu.VMEM((length, width), BF16)] * 3
        + [pltpu.VMEM((near, 8, HEAD), F32), pltpu.VMEM((far, 8, HEAD), F32)]
        + [dma((2,)), dma((4,))]
        + [dma((4, heads, shards - 1))] * 2
        + [dma((3, heads))] * 2
        + [dma((near - 1,))] * 2
        + [dma((far - 1,))] * 2,
        compiler_params=pltpu.CompilerParams(
            collective_id=0, has_side_effects=True, vmem_limit_bytes=63 * 1024 * 1024
        ),
        cost_estimate=pl.CostEstimate(
            flops=12 * heads * length * length * HEAD,
            bytes_accessed=16 * length * width,
            transcendentals=heads * length * length,
        ),
    )(query_in, key_in, value_in, latent_now, latent_next, gains, rewards, steps, counts)


def solution(mesh):
    sizes = tuple(mesh.shape[name] for name in ("segment", "dp", "seq"))
    rows = P(("segment", "dp"), "seq", None)
    columns = P(("segment", "dp"), None, "seq")
    return jax.shard_map(
        functools.partial(body, sizes),
        mesh=mesh,
        in_specs=(rows,) * 5 + (P(),) * 4,
        out_specs=(columns, columns, columns, P()),
        check_vma=False,
    )
```

```python
import functools

import jax
import jax.numpy as jnp
from jax import lax
from jax.experimental import pallas as pl
from jax.experimental.pallas import tpu as pltpu
from jax.sharding import PartitionSpec as P

HEAD = 128
STEPS = 16
GROUP = 16
AHEAD = 2
LOG2E = 1.4426950408889634
SCALE = HEAD ** -0.5
MESH = pl.DeviceIdType.MESH
F32 = jnp.float32
BF16 = jnp.bfloat16


def dot(a, b, da, db):
    return lax.dot_general(a, b, (((da,), (db,)), ((), ())), preferred_element_type=F32)


def unit_rows(x, average):
    wide = x.astype(F32)
    r = lax.rsqrt(dot((wide * wide).astype(BF16), average, 1, 0) + 1e-06)
    return wide * r, r


def unit_rows_back(grad, unit, r, gain, average):
    inner = grad * gain
    mean = dot((inner * unit).astype(BF16), average, 1, 0)
    return r * (inner - unit * mean), jnp.sum(grad * unit, axis=0, keepdims=True)


def head_grads(q_in, k_in, v, diff, consts, bias, row_scale, delta, average, ones):
    q_gain, k_gain, dq_gain, dk_gain = consts
    length = q_in.shape[0]
    q_unit, q_r = unit_rows(q_in, average)
    k_unit, k_r = unit_rows(k_in, average)
    q = (q_unit * q_gain).astype(BF16)
    k = (k_unit * k_gain).astype(BF16)
    raw = jnp.exp2(dot(q, k, 1, 1) + bias)
    weights = raw.astype(BF16)
    inverse = 1.0 / dot(weights, ones, 1, 0)
    velocity = dot(weights, v, 1, 0) * inverse
    cotangent = (row_scale * inverse * (diff.astype(F32) + delta * velocity)).astype(BF16)
    dv = dot(weights, cotangent, 0, 0)
    dw = dot(cotangent, v, 1, 1)
    inner = dot((cotangent.astype(F32) * velocity).astype(BF16), ones[:HEAD], 1, 0)
    ds = (raw * (dw - jnp.concatenate([inner] * (length // HEAD), axis=1))).astype(BF16)
    dk, dg_k = unit_rows_back(dot(ds, q, 0, 0), k_unit, k_r, dk_gain, average)
    dq, dg_q = unit_rows_back(dot(ds, k, 1, 0), q_unit, q_r, dq_gain, average)
    return dq.astype(BF16), dk.astype(BF16), dv.astype(BF16), dg_q, dg_k


def sigma(index):
    level = 1.0 - index.astype(F32) / STEPS
    return 7.0 * level / (1.0 + 6.0 * level)


def kernel(
    sizes,
    q_ref, k_ref, v_ref, now_ref, next_ref, gains_ref, reward_ref, step_ref, count_ref,
    oq_ref, ok_ref, ov_ref, og_ref,
    qb, kb, vb, db, lat, diff, gq, gk, gv, sum1, sum2,
    lat_sem, own_sem, send_sem, recv_sem, out_send, out_recv, s1_send, s1_recv, s2_send, s2_recv,
):
    segments, replicas, shards = sizes
    seg, dp, me = (lax.axis_index(name) for name in ("segment", "dp", "seq"))
    rows, width = q_ref.shape[1], qb.shape[1]
    heads = width // HEAD

    loads = [
        pltpu.make_async_copy(ref.at[0], lat.at[i], lat_sem.at[i])
        for i, ref in enumerate((now_ref, next_ref))
    ]
    for copy in loads:
        copy.start()

    sources = (q_ref.at[0], k_ref.at[0], v_ref.at[0], diff)
    targets = (qb, kb, vb, db)
    my_rows = pl.ds(pl.multiple_of(me * rows, rows), rows)
    own_columns = pl.ds(pl.multiple_of(me * width, width), width)
    own = [
        pltpu.make_async_copy(sources[i].at[:, own_columns], targets[i].at[my_rows, :], own_sem.at[i])
        for i in range(4)
    ]
    for copy in own[:3]:
        copy.start()

    group1 = [
        (lax.rem(seg + a, segments), dp, lax.rem(me + b, shards))
        for a in range(segments)
        for b in range(shards)
        if a or b
    ]
    group2 = [(seg, lax.rem(dp + a, replicas), me) for a in range(1, replicas)]
    barrier = pltpu.get_barrier_semaphore()
    for device in group1 + group2:
        pl.semaphore_signal(barrier, inc=1, device_id=device, device_id_type=MESH)
    pl.semaphore_wait(barrier, len(group1) + len(group2))

    def part(array, head, step):
        other = lax.rem(me + step, shards)
        columns = pl.ds(pl.multiple_of(other * width + head * HEAD, HEAD), HEAD)
        return pltpu.make_async_remote_copy(
            src_ref=sources[array].at[:, columns],
            dst_ref=targets[array].at[my_rows, pl.ds(head * HEAD, HEAD)],
            send_sem=send_sem.at[array, head, step - 1],
            recv_sem=recv_sem.at[array, head, step - 1],
            device_id=(seg, dp, other),
            device_id_type=MESH,
        )

    parts = [
        [[part(i, h, s) for s in range(1, shards)] for i in range(4)] for h in range(heads)
    ]

    def send(head, arrays):
        for i in arrays:
            for copy in parts[head][i]:
                copy.start()

    ahead = min(AHEAD, heads)
    send(0, (0, 1, 2))
    for copy in loads:
        copy.wait()
    full = diff.shape[1]
    for c in range(0, full, 256):
        cols = slice(c, c + 256)
        diff[:, cols] = (lat[1, :, cols].astype(F32) - lat[0, :, cols].astype(F32)).astype(BF16)
    send(0, (3,))
    for h in range(1, ahead):
        send(h, (0, 1, 2, 3))
    own[3].start()

    video = seg * replicas + dp
    first = video // GROUP * GROUP
    one = (1, 1)
    rewards = [reward_ref[first + i] for i in range(GROUP)]
    mean = sum(rewards[1:], rewards[0]) * F32(1.0 / GROUP)
    spread = sum((r - mean) * (r - mean) for r in rewards) * F32(1.0 / GROUP)
    spread = jnp.sqrt(jnp.full(one, spread, F32))
    advantage = jnp.full(one, reward_ref[video] - mean, F32) / jnp.maximum(spread, F32(0.25))
    step = jnp.full(one, step_ref[video], jnp.int32)
    delta = sigma(step) - sigma(step + 1)
    count = count_ref[video]
    q_gain, k_gain = gains_ref[0:1], gains_ref[1:2]
    consts = (
        q_gain * F32(SCALE * LOG2E), k_gain, q_gain * F32(SCALE), k_gain * F32(1.0 / LOG2E)
    )
    length = qb.shape[0]
    average = jnp.full((HEAD, HEAD), 1.0 / HEAD, BF16)
    ones = jnp.full((length, HEAD), 1.0, BF16)
    bias = jnp.where(
        lax.broadcasted_iota(jnp.int32, (1, length), 1) < count, F32(0.0), F32(-1e30)
    )
    row_scale = jnp.where(
        lax.broadcasted_iota(jnp.int32, (length, HEAD), 0) < count, advantage, F32(0.0)
    )

    for copy in own:
        copy.wait()

    next_device = (lax.rem(seg + 1, segments), dp, me)
    outs = []
    dg_q = jnp.zeros((1, HEAD), F32)
    dg_k = jnp.zeros((1, HEAD), F32)
    for h in range(heads):
        for i in range(4):
            for copy in parts[h][i]:
                copy.wait_recv()
        if h + ahead < heads:
            send(h + ahead, (0, 1, 2, 3))
        cols = slice(h * HEAD, (h + 1) * HEAD)
        dq, dk, dv, a, b = head_grads(
            qb[:, cols], kb[:, cols], vb[:, cols], db[:, cols],
            consts, bias, row_scale, delta, average, ones,
        )
        dg_q, dg_k = dg_q + a, dg_k + b
        gq[:, cols], gk[:, cols], gv[:, cols] = dq, dk, dv
        for i, (src, dst) in enumerate(((gq, oq_ref), (gk, ok_ref), (gv, ov_ref))):
            copy = pltpu.make_async_remote_copy(
                src_ref=src.at[:, cols],
                dst_ref=dst.at[0, :, cols],
                send_sem=out_send.at[i, h],
                recv_sem=out_recv.at[i, h],
                device_id=next_device,
                device_id_type=MESH,
            )
            copy.start()
            outs.append(copy)

    def spread_sum(slots, mine, value, group, sent, received):
        slots[mine] = value
        copies = [
            pltpu.make_async_remote_copy(
                src_ref=slots.at[mine],
                dst_ref=slots.at[mine],
                send_sem=sent.at[i],
                recv_sem=received.at[i],
                device_id=device,
                device_id_type=MESH,
            )
            for i, device in enumerate(group)
        ]
        for copy in copies:
            copy.start()
        for copy in copies:
            copy.wait_recv()
        total = slots[0]
        for i in range(1, len(group) + 1):
            total = total + slots[i]
        return total, copies

    share = jnp.concatenate([dg_q * F32(SCALE), dg_k * F32(1.0 / LOG2E), jnp.zeros((6, HEAD), F32)], axis=0)
    total, copies1 = spread_sum(sum1, seg * shards + me, share, group1, s1_send, s1_recv)
    total, copies2 = spread_sum(sum2, dp, total, group2, s2_send, s2_recv)
    og_ref[...] = total[0:2] * F32(1.0 / (segments * replicas))

    for copy in outs:
        copy.wait()
    for copy in copies1 + copies2:
        copy.wait_send()
    for head in parts:
        for array in head:
            for copy in array:
                copy.wait_send()


def hand_over(*refs):
    sems = refs[8]
    copies = [pltpu.make_async_copy(refs[i], refs[4 + i], sems.at[i]) for i in range(4)]
    for copy in copies:
        copy.start()
    for copy in copies:
        copy.wait()


def body(sizes, query_in, key_in, value_in, latent_now, latent_next, gains, rewards, steps, counts):
    segments, replicas, shards = sizes
    _, rows, full = query_in.shape
    length, width = rows * shards, full // shards
    heads = width // HEAD
    any_space = pl.BlockSpec(memory_space=pltpu.HBM)
    vmem = pl.BlockSpec(memory_space=pltpu.VMEM)
    smem = pl.BlockSpec(memory_space=pltpu.SMEM)
    grad = jax.ShapeDtypeStruct((1, length, width), BF16)
    near, far = segments * shards, replicas
    dma = pltpu.SemaphoreType.DMA
    results = pl.pallas_call(
        functools.partial(kernel, sizes),
        out_shape=(grad, grad, grad, jax.ShapeDtypeStruct((2, HEAD), F32)),
        in_specs=[any_space] * 5 + [vmem] + [smem] * 3,
        out_specs=(any_space, any_space, any_space, vmem),
        scratch_shapes=[pltpu.VMEM((length, width), BF16)] * 4
        + [pltpu.VMEM((2, rows, full), BF16), pltpu.VMEM((rows, full), BF16)]
        + [pltpu.VMEM((length, width), BF16)] * 3
        + [pltpu.VMEM((near, 8, HEAD), F32), pltpu.VMEM((far, 8, HEAD), F32)]
        + [dma((2,)), dma((4,))]
        + [dma((4, heads, shards - 1))] * 2
        + [dma((3, heads))] * 2
        + [dma((near - 1,))] * 2
        + [dma((far - 1,))] * 2,
        compiler_params=pltpu.CompilerParams(
            collective_id=0, has_side_effects=True, vmem_limit_bytes=63 * 1024 * 1024
        ),
        cost_estimate=pl.CostEstimate(
            flops=12 * heads * length * length * HEAD,
            bytes_accessed=16 * length * width,
            transcendentals=heads * length * length,
        ),
    )(query_in, key_in, value_in, latent_now, latent_next, gains, rewards, steps, counts)
    hbm = pl.BlockSpec(memory_space=pltpu.HBM)
    return pl.pallas_call(
        hand_over,
        out_shape=(grad, grad, grad, jax.ShapeDtypeStruct((2, HEAD), F32)),
        in_specs=[hbm] * 4,
        out_specs=(hbm,) * 4,
        scratch_shapes=[dma((4,))],
        compiler_params=pltpu.CompilerParams(vmem_limit_bytes=63 * 1024 * 1024),
    )(*results)


def solution(mesh):
    sizes = tuple(mesh.shape[name] for name in ("segment", "dp", "seq"))
    rows = P(("segment", "dp"), "seq", None)
    columns = P(("segment", "dp"), None, "seq")
    return jax.shard_map(
        functools.partial(body, sizes),
        mesh=mesh,
        in_specs=(rows,) * 5 + (P(),) * 4,
        out_specs=(columns, columns, columns, P()),
        check_vma=False,
    )
```

```python
import functools

import jax
import jax.numpy as jnp
from jax import lax
from jax.experimental import pallas as pl
from jax.experimental.pallas import tpu as pltpu
from jax.sharding import PartitionSpec as P

HEAD = 128
STEPS = 16
GROUP = 16
AHEAD = 2
LOG2E = 1.4426950408889634
SCALE = HEAD ** -0.5
MESH = pl.DeviceIdType.MESH
F32 = jnp.float32
BF16 = jnp.bfloat16


def dot(a, b, da, db):
    return lax.dot_general(a, b, (((da,), (db,)), ((), ())), preferred_element_type=F32)


def unit_rows(x, average):
    wide = x.astype(F32)
    r = lax.rsqrt(dot((wide * wide).astype(BF16), average, 1, 0) + 1e-06)
    return wide * r, r


def unit_rows_back(grad, unit, r, gain, average):
    inner = grad * gain
    mean = dot((inner * unit).astype(BF16), average, 1, 0)
    return r * (inner - unit * mean), jnp.sum(grad * unit, axis=0, keepdims=True)


def head_grads(q_in, k_in, v, diff, consts, bias, row_scale, delta, average, ones):
    q_gain, k_gain, dq_gain, dk_gain = consts
    length = q_in.shape[0]
    q_unit, q_r = unit_rows(q_in, average)
    k_unit, k_r = unit_rows(k_in, average)
    q = (q_unit * q_gain).astype(BF16)
    k = (k_unit * k_gain).astype(BF16)
    raw = jnp.exp2(dot(q, k, 1, 1) + bias)
    weights = raw.astype(BF16)
    inverse = 1.0 / dot(weights, ones, 1, 0)
    velocity = dot(weights, v, 1, 0) * inverse
    cotangent = (row_scale * inverse * (diff.astype(F32) + delta * velocity)).astype(BF16)
    dv = dot(weights, cotangent, 0, 0)
    dw = dot(cotangent, v, 1, 1)
    inner = dot((cotangent.astype(F32) * velocity).astype(BF16), ones[:HEAD], 1, 0)
    ds = (raw * (dw - jnp.concatenate([inner] * (length // HEAD), axis=1))).astype(BF16)
    dk, dg_k = unit_rows_back(dot(ds, q, 0, 0), k_unit, k_r, dk_gain, average)
    dq, dg_q = unit_rows_back(dot(ds, k, 1, 0), q_unit, q_r, dq_gain, average)
    return dq.astype(BF16), dk.astype(BF16), dv.astype(BF16), dg_q, dg_k


def sigma(index):
    level = 1.0 - index.astype(F32) / STEPS
    return 7.0 * level / (1.0 + 6.0 * level)


def kernel(
    sizes,
    q_ref, k_ref, v_ref, now_ref, next_ref, gains_ref, reward_ref, step_ref, count_ref,
    oq_ref, ok_ref, ov_ref, og_ref,
    qs, ks, vs, qb, kb, vb, db, lat, diff, gq, gk, gv, rq, rk, rv, sum1, sum2,
    load_sem, store_sem, send_sem, recv_sem, out_send, out_recv, s1_send, s1_recv, s2_send, s2_recv,
):
    segments, replicas, shards = sizes
    seg, dp, me = (lax.axis_index(name) for name in ("segment", "dp", "seq"))
    rows, width = q_ref.shape[1], qb.shape[1]
    heads = width // HEAD

    loads = [
        pltpu.make_async_copy(ref.at[0], dst, load_sem.at[i])
        for i, (ref, dst) in enumerate(
            ((q_ref, qs), (k_ref, ks), (v_ref, vs), (now_ref, lat.at[0]), (next_ref, lat.at[1]))
        )
    ]
    for copy in loads:
        copy.start()

    sources = (qs, ks, vs, diff)
    targets = (qb, kb, vb, db)
    my_rows = pl.ds(pl.multiple_of(me * rows, rows), rows)
    own_columns = pl.ds(pl.multiple_of(me * width, width), width)

    group1 = [
        (lax.rem(seg + a, segments), dp, lax.rem(me + b, shards))
        for a in range(segments)
        for b in range(shards)
        if a or b
    ]
    group2 = [(seg, lax.rem(dp + a, replicas), me) for a in range(1, replicas)]
    barrier = pltpu.get_barrier_semaphore()
    for device in group1 + group2:
        pl.semaphore_signal(barrier, inc=1, device_id=device, device_id_type=MESH)
    pl.semaphore_wait(barrier, len(group1) + len(group2))

    def part(array, head, step):
        other = lax.rem(me + step, shards)
        columns = pl.ds(pl.multiple_of(other * width + head * HEAD, HEAD), HEAD)
        return pltpu.make_async_remote_copy(
            src_ref=sources[array].at[:, columns],
            dst_ref=targets[array].at[my_rows, pl.ds(head * HEAD, HEAD)],
            send_sem=send_sem.at[array, head, step - 1],
            recv_sem=recv_sem.at[array, head, step - 1],
            device_id=(seg, dp, other),
            device_id_type=MESH,
        )

    parts = [
        [[part(i, h, s) for s in range(1, shards)] for i in range(4)] for h in range(heads)
    ]

    def send(head, arrays):
        for i in arrays:
            for copy in parts[head][i]:
                copy.start()

    ahead = min(AHEAD, heads)
    for i in range(3):
        loads[i].wait()
        send(0, (i,))
    for copy in loads[3:]:
        copy.wait()
    full = diff.shape[1]
    for c in range(0, full, 256):
        cols = slice(c, c + 256)
        diff[:, cols] = (lat[1, :, cols].astype(F32) - lat[0, :, cols].astype(F32)).astype(BF16)
    send(0, (3,))
    for h in range(1, ahead):
        send(h, (0, 1, 2, 3))
    for source, target in zip(sources, targets):
        target[my_rows, :] = source[:, own_columns]

    video = seg * replicas + dp
    first = video // GROUP * GROUP
    one = (1, 1)
    rewards = [reward_ref[first + i] for i in range(GROUP)]
    mean = sum(rewards[1:], rewards[0]) * F32(1.0 / GROUP)
    spread = sum((r - mean) * (r - mean) for r in rewards) * F32(1.0 / GROUP)
    spread = jnp.sqrt(jnp.full(one, spread, F32))
    advantage = jnp.full(one, reward_ref[video] - mean, F32) / jnp.maximum(spread, F32(0.25))
    step = jnp.full(one, step_ref[video], jnp.int32)
    delta = sigma(step) - sigma(step + 1)
    count = count_ref[video]
    q_gain, k_gain = gains_ref[0:1], gains_ref[1:2]
    consts = (
        q_gain * F32(SCALE * LOG2E), k_gain, q_gain * F32(SCALE), k_gain * F32(1.0 / LOG2E)
    )
    length = qb.shape[0]
    average = jnp.full((HEAD, HEAD), 1.0 / HEAD, BF16)
    ones = jnp.full((length, HEAD), 1.0, BF16)
    bias = jnp.where(
        lax.broadcasted_iota(jnp.int32, (1, length), 1) < count, F32(0.0), F32(-1e30)
    )
    row_scale = jnp.where(
        lax.broadcasted_iota(jnp.int32, (length, HEAD), 0) < count, advantage, F32(0.0)
    )

    next_device = (lax.rem(seg + 1, segments), dp, me)
    outs, stores = [], []
    dg_q = jnp.zeros((1, HEAD), F32)
    dg_k = jnp.zeros((1, HEAD), F32)

    def store(head):
        cols = slice(head * HEAD, (head + 1) * HEAD)
        for i, (src, dst) in enumerate(((rq, oq_ref), (rk, ok_ref), (rv, ov_ref))):
            outs[head][i].wait_recv()
            copy = pltpu.make_async_copy(
                src.at[:, cols], dst.at[0, :, cols], store_sem.at[i, head]
            )
            copy.start()
            stores.append(copy)

    for h in range(heads):
        for i in range(4):
            for copy in parts[h][i]:
                copy.wait_recv()
        if h + ahead < heads:
            send(h + ahead, (0, 1, 2, 3))
        cols = slice(h * HEAD, (h + 1) * HEAD)
        dq, dk, dv, a, b = head_grads(
            qb[:, cols], kb[:, cols], vb[:, cols], db[:, cols],
            consts, bias, row_scale, delta, average, ones,
        )
        dg_q, dg_k = dg_q + a, dg_k + b
        gq[:, cols], gk[:, cols], gv[:, cols] = dq, dk, dv
        head_outs = []
        for i, (src, dst) in enumerate(((gq, rq), (gk, rk), (gv, rv))):
            copy = pltpu.make_async_remote_copy(
                src_ref=src.at[:, cols],
                dst_ref=dst.at[:, cols],
                send_sem=out_send.at[i, h],
                recv_sem=out_recv.at[i, h],
                device_id=next_device,
                device_id_type=MESH,
            )
            copy.start()
            head_outs.append(copy)
        outs.append(head_outs)
        if h >= 1:
            store(h - 1)

    def spread_sum(slots, mine, value, group, sent, received):
        slots[mine] = value
        copies = [
            pltpu.make_async_remote_copy(
                src_ref=slots.at[mine],
                dst_ref=slots.at[mine],
                send_sem=sent.at[i],
                recv_sem=received.at[i],
                device_id=device,
                device_id_type=MESH,
            )
            for i, device in enumerate(group)
        ]
        for copy in copies:
            copy.start()
        for copy in copies:
            copy.wait_recv()
        total = slots[0]
        for i in range(1, len(group) + 1):
            total = total + slots[i]
        return total, copies

    share = jnp.concatenate([dg_q * F32(SCALE), dg_k * F32(1.0 / LOG2E), jnp.zeros((6, HEAD), F32)], axis=0)
    total, copies1 = spread_sum(sum1, seg * shards + me, share, group1, s1_send, s1_recv)
    total, copies2 = spread_sum(sum2, dp, total, group2, s2_send, s2_recv)
    og_ref[...] = total[0:2] * F32(1.0 / (segments * replicas))

    store(heads - 1)
    for head in outs:
        for copy in head:
            copy.wait_send()
    for copy in stores:
        copy.wait()
    for copy in copies1 + copies2:
        copy.wait_send()
    for head in parts:
        for array in head:
            for copy in array:
                copy.wait_send()


def hand_over(pieces, *refs):
    ins, outs, holds, sums, in_sem, out_sem = refs[:4], refs[4:8], refs[8:11], refs[11], refs[12], refs[13]
    rows = ins[0].shape[1] // pieces
    todo = []
    for p in range(pieces):
        part = pl.ds(p * rows, rows)
        for i in range(3):
            hold = holds[i].at[part]
            todo.append((
                pltpu.make_async_copy(ins[i].at[0, part], hold, in_sem.at[i, p]),
                pltpu.make_async_copy(hold, outs[i].at[0, part], out_sem.at[i, p]),
            ))
    todo.append((
        pltpu.make_async_copy(ins[3], sums, in_sem.at[3, 0]),
        pltpu.make_async_copy(sums, outs[3], out_sem.at[3, 0]),
    ))
    for load, _ in todo:
        load.start()
    for load, store in todo:
        load.wait()
        store.start()
    for _, store in todo:
        store.wait()


def body(sizes, query_in, key_in, value_in, latent_now, latent_next, gains, rewards, steps, counts):
    segments, replicas, shards = sizes
    _, rows, full = query_in.shape
    length, width = rows * shards, full // shards
    heads = width // HEAD
    any_space = pl.BlockSpec(memory_space=pltpu.HBM)
    vmem = pl.BlockSpec(memory_space=pltpu.VMEM)
    smem = pl.BlockSpec(memory_space=pltpu.SMEM)
    grad = jax.ShapeDtypeStruct((1, length, width), BF16)
    near, far = segments * shards, replicas
    dma = pltpu.SemaphoreType.DMA
    results = pl.pallas_call(
        functools.partial(kernel, sizes),
        out_shape=(grad, grad, grad, jax.ShapeDtypeStruct((2, HEAD), F32)),
        in_specs=[any_space] * 5 + [vmem] + [smem] * 3,
        out_specs=(any_space, any_space, any_space, vmem),
        scratch_shapes=[pltpu.VMEM((rows, full), BF16)] * 3
        + [pltpu.VMEM((length, width), BF16)] * 4
        + [pltpu.VMEM((2, rows, full), BF16), pltpu.VMEM((rows, full), BF16)]
        + [pltpu.VMEM((length, width), BF16)] * 6
        + [pltpu.VMEM((near, 8, HEAD), F32), pltpu.VMEM((far, 8, HEAD), F32)]
        + [dma((5,)), dma((3, heads))]
        + [dma((4, heads, shards - 1))] * 2
        + [dma((3, heads))] * 2
        + [dma((near - 1,))] * 2
        + [dma((far - 1,))] * 2,
        compiler_params=pltpu.CompilerParams(
            collective_id=0, has_side_effects=True, vmem_limit_bytes=63 * 1024 * 1024
        ),
        cost_estimate=pl.CostEstimate(
            flops=12 * heads * length * length * HEAD,
            bytes_accessed=16 * length * width,
            transcendentals=heads * length * length,
        ),
    )(query_in, key_in, value_in, latent_now, latent_next, gains, rewards, steps, counts)
    hbm = pl.BlockSpec(memory_space=pltpu.HBM)
    return pl.pallas_call(
        functools.partial(hand_over, 2),
        out_shape=(grad, grad, grad, jax.ShapeDtypeStruct((2, HEAD), F32)),
        in_specs=[hbm] * 4,
        out_specs=(hbm,) * 4,
        scratch_shapes=[pltpu.VMEM((length, width), BF16)] * 3
        + [pltpu.VMEM((2, HEAD), F32), dma((4, 2)), dma((4, 2))],
        compiler_params=pltpu.CompilerParams(vmem_limit_bytes=63 * 1024 * 1024),
    )(*results)


def solution(mesh):
    sizes = tuple(mesh.shape[name] for name in ("segment", "dp", "seq"))
    rows = P(("segment", "dp"), "seq", None)
    columns = P(("segment", "dp"), None, "seq")
    return jax.shard_map(
        functools.partial(body, sizes),
        mesh=mesh,
        in_specs=(rows,) * 5 + (P(),) * 4,
        out_specs=(columns, columns, columns, P()),
        check_vma=False,
    )
```

```python
import functools

import jax
import jax.numpy as jnp
from jax import lax
from jax.experimental import pallas as pl
from jax.experimental.pallas import tpu as pltpu
from jax.sharding import PartitionSpec as P

HEAD = 128
STEPS = 16
GROUP = 16
AHEAD = 2
LOG2E = 1.4426950408889634
SCALE = HEAD ** -0.5
MESH = pl.DeviceIdType.MESH
F32 = jnp.float32
BF16 = jnp.bfloat16


def dot(a, b, da, db):
    return lax.dot_general(a, b, (((da,), (db,)), ((), ())), preferred_element_type=F32)


def unit_rows(x, average):
    wide = x.astype(F32)
    r = lax.rsqrt(dot((wide * wide).astype(BF16), average, 1, 0) + 1e-06)
    return wide * r, r


def unit_rows_back(grad, unit, r, gain, average):
    inner = grad * gain
    mean = dot((inner * unit).astype(BF16), average, 1, 0)
    return r * (inner - unit * mean), jnp.sum(grad * unit, axis=0, keepdims=True)


def head_grads(q_in, k_in, v, diff, consts, bias, row_scale, delta, average, ones):
    q_gain, k_gain, dq_gain, dk_gain = consts
    length = q_in.shape[0]
    q_unit, q_r = unit_rows(q_in, average)
    k_unit, k_r = unit_rows(k_in, average)
    q = (q_unit * q_gain).astype(BF16)
    k = (k_unit * k_gain).astype(BF16)
    raw = jnp.exp2(dot(q, k, 1, 1) + bias)
    weights = raw.astype(BF16)
    inverse = 1.0 / dot(weights, ones, 1, 0)
    velocity = dot(weights, v, 1, 0) * inverse
    cotangent = (row_scale * inverse * (diff.astype(F32) + delta * velocity)).astype(BF16)
    dv = dot(weights, cotangent, 0, 0)
    dw = dot(cotangent, v, 1, 1)
    inner = dot((cotangent.astype(F32) * velocity).astype(BF16), ones[:HEAD], 1, 0)
    ds = (raw * (dw - jnp.concatenate([inner] * (length // HEAD), axis=1))).astype(BF16)
    dk, dg_k = unit_rows_back(dot(ds, q, 0, 0), k_unit, k_r, dk_gain, average)
    dq, dg_q = unit_rows_back(dot(ds, k, 1, 0), q_unit, q_r, dq_gain, average)
    return dq.astype(BF16), dk.astype(BF16), dv.astype(BF16), dg_q, dg_k


def sigma(index):
    level = 1.0 - index.astype(F32) / STEPS
    return 7.0 * level / (1.0 + 6.0 * level)


def kernel(
    sizes,
    q_ref, k_ref, v_ref, now_ref, next_ref, gains_ref, reward_ref, step_ref, count_ref,
    oq_ref, ok_ref, ov_ref, og_ref,
    qs, ks, vs, qb, kb, vb, db, lat, diff, gq, gk, gv, rq, rk, rv, sum1, sum2,
    load_sem, store_sem, send_sem, recv_sem, out_send, out_recv, s1_send, s1_recv, s2_send, s2_recv,
):
    segments, replicas, shards = sizes
    seg, dp, me = (lax.axis_index(name) for name in ("segment", "dp", "seq"))
    rows, heads = q_ref.shape[1], qb.shape[0]
    width = heads * HEAD

    loads = [
        pltpu.make_async_copy(ref.at[0], dst, load_sem.at[i])
        for i, (ref, dst) in enumerate(
            ((q_ref, qs), (k_ref, ks), (v_ref, vs), (now_ref, lat.at[0]), (next_ref, lat.at[1]))
        )
    ]
    for copy in loads:
        copy.start()

    sources = (qs, ks, vs, diff)
    targets = (qb, kb, vb, db)
    my_rows = pl.ds(pl.multiple_of(me * rows, rows), rows)

    group1 = [
        (lax.rem(seg + a, segments), dp, lax.rem(me + b, shards))
        for a in range(segments)
        for b in range(shards)
        if a or b
    ]
    group2 = [(seg, lax.rem(dp + a, replicas), me) for a in range(1, replicas)]
    barrier = pltpu.get_barrier_semaphore()
    for device in group1 + group2:
        pl.semaphore_signal(barrier, inc=1, device_id=device, device_id_type=MESH)
    pl.semaphore_wait(barrier, len(group1) + len(group2))

    def part(array, head, step):
        other = lax.rem(me + step, shards)
        columns = pl.ds(pl.multiple_of(other * width + head * HEAD, HEAD), HEAD)
        return pltpu.make_async_remote_copy(
            src_ref=sources[array].at[:, columns],
            dst_ref=targets[array].at[head, my_rows],
            send_sem=send_sem.at[array, head, step - 1],
            recv_sem=recv_sem.at[array, head, step - 1],
            device_id=(seg, dp, other),
            device_id_type=MESH,
        )

    def parts(head, arrays=(0, 1, 2, 3)):
        return [part(i, head, s) for i in arrays for s in range(1, shards)]

    def send(head, arrays=(0, 1, 2, 3)):
        for copy in parts(head, arrays):
            copy.start()

    ahead = min(AHEAD, heads)
    for i in range(3):
        loads[i].wait()
        send(0, (i,))
    for copy in loads[3:]:
        copy.wait()
    full = diff.shape[1]
    for c in range(0, full, 256):
        cols = slice(c, c + 256)
        diff[:, cols] = (lat[1, :, cols].astype(F32) - lat[0, :, cols].astype(F32)).astype(BF16)
    send(0, (3,))
    for h in range(1, ahead):
        send(h)

    video = seg * replicas + dp
    first = video // GROUP * GROUP
    one = (1, 1)
    rewards = [reward_ref[first + i] for i in range(GROUP)]
    mean = sum(rewards[1:], rewards[0]) * F32(1.0 / GROUP)
    spread = sum((r - mean) * (r - mean) for r in rewards) * F32(1.0 / GROUP)
    spread = jnp.sqrt(jnp.full(one, spread, F32))
    advantage = jnp.full(one, reward_ref[video] - mean, F32) / jnp.maximum(spread, F32(0.25))
    step = jnp.full(one, step_ref[video], jnp.int32)
    delta = sigma(step) - sigma(step + 1)
    count = count_ref[video]
    q_gain, k_gain = gains_ref[0:1], gains_ref[1:2]
    consts = (
        q_gain * F32(SCALE * LOG2E), k_gain, q_gain * F32(SCALE), k_gain * F32(1.0 / LOG2E)
    )
    length = qb.shape[1]
    average = jnp.full((HEAD, HEAD), 1.0 / HEAD, BF16)
    ones = jnp.full((length, HEAD), 1.0, BF16)
    bias = jnp.where(
        lax.broadcasted_iota(jnp.int32, (1, length), 1) < count, F32(0.0), F32(-1e30)
    )
    row_scale = jnp.where(
        lax.broadcasted_iota(jnp.int32, (length, HEAD), 0) < count, advantage, F32(0.0)
    )

    next_device = (lax.rem(seg + 1, segments), dp, me)
    grads = ((gq, rq, oq_ref), (gk, rk, ok_ref), (gv, rv, ov_ref))

    def outs(head):
        return [
            pltpu.make_async_remote_copy(
                src_ref=src.at[head],
                dst_ref=dst.at[head],
                send_sem=out_send.at[i, head],
                recv_sem=out_recv.at[i, head],
                device_id=next_device,
                device_id_type=MESH,
            )
            for i, (src, dst, _) in enumerate(grads)
        ]

    def stores(head):
        cols = pl.ds(pl.multiple_of(head * HEAD, HEAD), HEAD)
        return [
            pltpu.make_async_copy(src.at[head], dst.at[0, :, cols], store_sem.at[i, head])
            for i, (_, src, dst) in enumerate(grads)
        ]

    def store(head):
        for copy, onward in zip(outs(head), stores(head)):
            copy.wait_recv()
            onward.start()

    def one_head(h, sums):
        own = pl.ds(pl.multiple_of(me * width + h * HEAD, HEAD), HEAD)
        for source, target in zip(sources, targets):
            target[h, my_rows] = source[:, own]
        for copy in parts(h):
            copy.wait_recv()

        @pl.when(h + ahead < heads)
        def _():
            send(h + ahead)

        dq, dk, dv, dg_q, dg_k = head_grads(
            qb[h], kb[h], vb[h], db[h], consts, bias, row_scale, delta, average, ones
        )
        gq[h], gk[h], gv[h] = dq, dk, dv
        for copy in outs(h):
            copy.start()

        @pl.when(h >= 1)
        def _():
            store(h - 1)

        return sums[0] + dg_q, sums[1] + dg_k

    zero = jnp.zeros((1, HEAD), F32)
    dg_q, dg_k = lax.fori_loop(0, heads, one_head, (zero, zero))

    def spread_sum(slots, mine, value, group, sent, received):
        slots[mine] = value
        copies = [
            pltpu.make_async_remote_copy(
                src_ref=slots.at[mine],
                dst_ref=slots.at[mine],
                send_sem=sent.at[i],
                recv_sem=received.at[i],
                device_id=device,
                device_id_type=MESH,
            )
            for i, device in enumerate(group)
        ]
        for copy in copies:
            copy.start()
        for copy in copies:
            copy.wait_recv()
        total = slots[0]
        for i in range(1, len(group) + 1):
            total = total + slots[i]
        return total, copies

    share = jnp.concatenate([dg_q * F32(SCALE), dg_k * F32(1.0 / LOG2E), jnp.zeros((6, HEAD), F32)], axis=0)
    total, copies1 = spread_sum(sum1, seg * shards + me, share, group1, s1_send, s1_recv)
    total, copies2 = spread_sum(sum2, dp, total, group2, s2_send, s2_recv)
    og_ref[...] = total[0:2] * F32(1.0 / (segments * replicas))

    store(heads - 1)
    for copy in copies1 + copies2:
        copy.wait_send()

    @pl.loop(0, heads)
    def _(h):
        for copy in outs(h) + parts(h):
            copy.wait_send()
        for copy in stores(h):
            copy.wait()


def hand_over(pieces, *refs):
    ins, outs, holds, sums, in_sem, out_sem = refs[:4], refs[4:8], refs[8:11], refs[11], refs[12], refs[13]
    rows = ins[0].shape[1] // pieces
    todo = []
    for p in range(pieces):
        part = pl.ds(p * rows, rows)
        for i in range(3):
            hold = holds[i].at[part]
            todo.append((
                pltpu.make_async_copy(ins[i].at[0, part], hold, in_sem.at[i, p]),
                pltpu.make_async_copy(hold, outs[i].at[0, part], out_sem.at[i, p]),
            ))
    todo.append((
        pltpu.make_async_copy(ins[3], sums, in_sem.at[3, 0]),
        pltpu.make_async_copy(sums, outs[3], out_sem.at[3, 0]),
    ))
    for load, _ in todo:
        load.start()
    for load, store in todo:
        load.wait()
        store.start()
    for _, store in todo:
        store.wait()


def body(sizes, query_in, key_in, value_in, latent_now, latent_next, gains, rewards, steps, counts):
    segments, replicas, shards = sizes
    _, rows, full = query_in.shape
    length, width = rows * shards, full // shards
    heads = width // HEAD
    any_space = pl.BlockSpec(memory_space=pltpu.HBM)
    vmem = pl.BlockSpec(memory_space=pltpu.VMEM)
    smem = pl.BlockSpec(memory_space=pltpu.SMEM)
    grad = jax.ShapeDtypeStruct((1, length, width), BF16)
    near, far = segments * shards, replicas
    dma = pltpu.SemaphoreType.DMA
    results = pl.pallas_call(
        functools.partial(kernel, sizes),
        out_shape=(grad, grad, grad, jax.ShapeDtypeStruct((2, HEAD), F32)),
        in_specs=[any_space] * 5 + [vmem] + [smem] * 3,
        out_specs=(any_space, any_space, any_space, vmem),
        scratch_shapes=[pltpu.VMEM((rows, full), BF16)] * 3
        + [pltpu.VMEM((heads, length, HEAD), BF16)] * 4
        + [pltpu.VMEM((2, rows, full), BF16), pltpu.VMEM((rows, full), BF16)]
        + [pltpu.VMEM((heads, length, HEAD), BF16)] * 6
        + [pltpu.VMEM((near, 8, HEAD), F32), pltpu.VMEM((far, 8, HEAD), F32)]
        + [dma((5,)), dma((3, heads))]
        + [dma((4, heads, shards - 1))] * 2
        + [dma((3, heads))] * 2
        + [dma((near - 1,))] * 2
        + [dma((far - 1,))] * 2,
        compiler_params=pltpu.CompilerParams(
            collective_id=0, has_side_effects=True, vmem_limit_bytes=63 * 1024 * 1024
        ),
        cost_estimate=pl.CostEstimate(
            flops=12 * heads * length * length * HEAD,
            bytes_accessed=16 * length * width,
            transcendentals=heads * length * length,
        ),
    )(query_in, key_in, value_in, latent_now, latent_next, gains, rewards, steps, counts)
    hbm = pl.BlockSpec(memory_space=pltpu.HBM)
    return pl.pallas_call(
        functools.partial(hand_over, 2),
        out_shape=(grad, grad, grad, jax.ShapeDtypeStruct((2, HEAD), F32)),
        in_specs=[hbm] * 4,
        out_specs=(hbm,) * 4,
        scratch_shapes=[pltpu.VMEM((length, width), BF16)] * 3
        + [pltpu.VMEM((2, HEAD), F32), dma((4, 2)), dma((4, 2))],
        compiler_params=pltpu.CompilerParams(vmem_limit_bytes=63 * 1024 * 1024),
    )(*results)


def solution(mesh):
    sizes = tuple(mesh.shape[name] for name in ("segment", "dp", "seq"))
    rows = P(("segment", "dp"), "seq", None)
    columns = P(("segment", "dp"), None, "seq")
    return jax.shard_map(
        functools.partial(body, sizes),
        mesh=mesh,
        in_specs=(rows,) * 5 + (P(),) * 4,
        out_specs=(columns, columns, columns, P()),
        check_vma=False,
    )
```

```python
import functools

import jax
import jax.numpy as jnp
from jax import lax
from jax.experimental import pallas as pl
from jax.experimental.pallas import tpu as pltpu
from jax.sharding import PartitionSpec as P

HEAD = 128
STEPS = 16
GROUP = 16
AHEAD = 2
LOG2E = 1.4426950408889634
SCALE = HEAD ** -0.5
MESH = pl.DeviceIdType.MESH
F32 = jnp.float32
BF16 = jnp.bfloat16


def dot(a, b, da, db):
    return lax.dot_general(a, b, (((da,), (db,)), ((), ())), preferred_element_type=F32)


def inverse_rms(wide, average):
    return lax.rsqrt(dot((wide * wide).astype(BF16), average, 1, 0) + 1e-06)


def unit_rows_back(grad, unit, r, gain, average):
    inner = grad * gain
    mean = dot((inner * unit).astype(BF16), average, 1, 0)
    return r * (inner - unit * mean), jnp.sum(grad * unit, axis=0, keepdims=True)


def sigma(index):
    level = 1.0 - index.astype(F32) / STEPS
    return 7.0 * level / (1.0 + 6.0 * level)


def kernel(
    sizes,
    q_ref, k_ref, v_ref, now_ref, next_ref, gains_ref, reward_ref, step_ref, count_ref,
    oq_ref, ok_ref, ov_ref, og_ref,
    qs, ks, vs, qb, kb, vb, db, lat, diff, gq, gk, gv, rq, rk, rv, sum1, sum2,
    load_sem, store_sem, send_sem, recv_sem, out_send, out_recv, s1_send, s1_recv, s2_send, s2_recv,
):
    segments, replicas, shards = sizes
    seg, dp, me = (lax.axis_index(name) for name in ("segment", "dp", "seq"))
    rows, heads = q_ref.shape[1], qb.shape[0]
    width = heads * HEAD

    loads = [
        pltpu.make_async_copy(ref.at[0], dst, load_sem.at[i])
        for i, (ref, dst) in enumerate(
            ((q_ref, qs), (k_ref, ks), (v_ref, vs), (now_ref, lat.at[0]), (next_ref, lat.at[1]))
        )
    ]
    for copy in loads:
        copy.start()

    sources = (qs, ks, vs, diff)
    targets = (qb, kb, vb, db)
    my_rows = pl.ds(pl.multiple_of(me * rows, rows), rows)

    group1 = [
        (lax.rem(seg + a, segments), dp, lax.rem(me + b, shards))
        for a in range(segments)
        for b in range(shards)
        if a or b
    ]
    group2 = [(seg, lax.rem(dp + a, replicas), me) for a in range(1, replicas)]
    barrier = pltpu.get_barrier_semaphore()
    for device in group1 + group2:
        pl.semaphore_signal(barrier, inc=1, device_id=device, device_id_type=MESH)
    pl.semaphore_wait(barrier, len(group1) + len(group2))

    def part(array, head, step):
        other = lax.rem(me + step, shards)
        columns = pl.ds(pl.multiple_of(other * width + head * HEAD, HEAD), HEAD)
        return pltpu.make_async_remote_copy(
            src_ref=sources[array].at[:, columns],
            dst_ref=targets[array].at[head, my_rows],
            send_sem=send_sem.at[array, head, step - 1],
            recv_sem=recv_sem.at[array, head, step - 1],
            device_id=(seg, dp, other),
            device_id_type=MESH,
        )

    def parts(head, arrays=(0, 1, 2, 3)):
        return [part(i, head, s) for i in arrays for s in range(1, shards)]

    def send(head, arrays=(0, 1, 2, 3)):
        for copy in parts(head, arrays):
            copy.start()

    together = next(n for n in (2, 1) if heads % n == 0)
    groups = heads // together
    ahead = min(AHEAD, groups)

    def send_group(g, arrays=(0, 1, 2, 3)):
        for i in arrays:
            for j in range(together):
                send(g * together + j, (i,))

    for i in range(3):
        loads[i].wait()
        send_group(0, (i,))
    for copy in loads[3:]:
        copy.wait()
    full = diff.shape[1]
    for c in range(0, full, 256):
        cols = slice(c, c + 256)
        diff[:, cols] = (lat[1, :, cols].astype(F32) - lat[0, :, cols].astype(F32)).astype(BF16)
    send_group(0, (3,))
    for g in range(1, ahead):
        send_group(g)

    video = seg * replicas + dp
    first = video // GROUP * GROUP
    one = (1, 1)
    rewards = [reward_ref[first + i] for i in range(GROUP)]
    mean = sum(rewards[1:], rewards[0]) * F32(1.0 / GROUP)
    spread = sum((r - mean) * (r - mean) for r in rewards) * F32(1.0 / GROUP)
    spread = jnp.sqrt(jnp.full(one, spread, F32))
    advantage = jnp.full(one, reward_ref[video] - mean, F32) / jnp.maximum(spread, F32(0.25))
    step = jnp.full(one, step_ref[video], jnp.int32)
    delta = sigma(step) - sigma(step + 1)
    count = count_ref[video]
    q_gain, k_gain = gains_ref[0:1], gains_ref[1:2]
    q_gain_log2 = q_gain * F32(SCALE * LOG2E)
    dq_gain, dk_gain = q_gain * F32(SCALE), k_gain * F32(1.0 / LOG2E)
    length = qb.shape[1]
    average = jnp.full((HEAD, HEAD), 1.0 / HEAD, BF16)
    ones = jnp.full((length, HEAD), 1.0, BF16)
    valid = lax.broadcasted_iota(jnp.int32, (length, HEAD), 0) < count
    row_scale = jnp.where(valid, advantage, F32(0.0))
    valid_ones = jnp.where(valid, F32(1.0), F32(0.0)).astype(BF16)

    def wide_lanes(x):
        return jnp.concatenate([x] * (length // HEAD), axis=1)

    next_device = (lax.rem(seg + 1, segments), dp, me)
    grads = ((gq, rq, oq_ref), (gk, rk, ok_ref), (gv, rv, ov_ref))

    def outs(head):
        return [
            pltpu.make_async_remote_copy(
                src_ref=src.at[head],
                dst_ref=dst.at[head],
                send_sem=out_send.at[i, head],
                recv_sem=out_recv.at[i, head],
                device_id=next_device,
                device_id_type=MESH,
            )
            for i, (src, dst, _) in enumerate(grads)
        ]

    def stores(head):
        cols = pl.ds(pl.multiple_of(head * HEAD, HEAD), HEAD)
        return [
            pltpu.make_async_copy(src.at[head], dst.at[0, :, cols], store_sem.at[i, head])
            for i, (_, src, dst) in enumerate(grads)
        ]

    def store(head):
        for copy, onward in zip(outs(head), stores(head)):
            copy.wait_recv()
            onward.start()

    def wait(hs, array):
        for h in hs:
            for copy in parts(h, (array,)):
                copy.wait_recv()

    def one_group(g, sums):
        hs = [g * together + j for j in range(together)]
        for h in hs:
            own = pl.ds(pl.multiple_of(me * width + h * HEAD, HEAD), HEAD)
            for source, target in zip(sources, targets):
                target[h, my_rows] = source[:, own]
        wait(hs, 0)

        @pl.when(g + ahead < groups)
        def _():
            send_group(g + ahead)

        wait(hs, 1)
        q_wide = [qb[h].astype(F32) for h in hs]
        k_wide = [kb[h].astype(F32) for h in hs]
        q_r = [inverse_rms(x, average) for x in q_wide]
        k_r = [jnp.where(valid, inverse_rms(x, average), F32(0.0)) for x in k_wide]
        q_unit = [x * r for x, r in zip(q_wide, q_r)]
        k_unit = [x * r for x, r in zip(k_wide, k_r)]
        q = [(x * q_gain_log2).astype(BF16) for x in q_unit]
        k = [(x * k_gain).astype(BF16) for x in k_unit]
        raw = [jnp.exp2(dot(a, b, 1, 1)) for a, b in zip(q, k)]
        weights = [x.astype(BF16) for x in raw]
        inverse = [1.0 / dot(x, valid_ones, 1, 0) for x in weights]
        raw_by_key = [jnp.exp2(dot(a, b, 1, 1)) for a, b in zip(k, q)]
        weights_by_key = [x.astype(BF16) for x in raw_by_key]
        wait(hs, 2)
        v = [vb[h] * valid_ones for h in hs]
        velocity = [dot(x, y, 1, 0) * z for x, y, z in zip(weights, v, inverse)]
        wait(hs, 3)
        cotangent = [
            (row_scale * z * (db[h].astype(F32) + delta * x)).astype(BF16)
            for h, x, z in zip(hs, velocity, inverse)
        ]
        for h, x, y in zip(hs, weights_by_key, cotangent):
            gv[h] = jnp.where(valid, dot(x, y, 1, 0), F32(0.0)).astype(BF16)
        along = [(x.astype(F32) * y).astype(BF16) for x, y in zip(cotangent, velocity)]
        inner = [dot(x, ones[:HEAD], 1, 0) for x in along]
        inner_by_key = [dot(ones, x, 1, 1) for x in along]
        ds_by_key = [
            (z * (dot(x, y, 1, 1) - i)).astype(BF16)
            for x, y, z, i in zip(v, cotangent, raw_by_key, inner_by_key)
        ]
        ds = [
            (z * (dot(y, x, 1, 1) - wide_lanes(i))).astype(BF16)
            for x, y, z, i in zip(v, cotangent, raw, inner)
        ]
        dk = [
            unit_rows_back(dot(x, y, 1, 0), u, r, dk_gain, average)
            for x, y, u, r in zip(ds_by_key, q, k_unit, k_r)
        ]
        dq = [
            unit_rows_back(dot(x, y, 1, 0), u, r, dq_gain, average)
            for x, y, u, r in zip(ds, k, q_unit, q_r)
        ]
        for h, x, y in zip(hs, dq, dk):
            gq[h], gk[h] = x[0].astype(BF16), y[0].astype(BF16)
        for h in hs:
            for copy in outs(h):
                copy.start()

        @pl.when(g >= 1)
        def _():
            for h in hs:
                store(h - together)

        return sum((x[1] for x in dq), sums[0]), sum((x[1] for x in dk), sums[1])

    zero = jnp.zeros((1, HEAD), F32)
    dg_q, dg_k = lax.fori_loop(0, groups, one_group, (zero, zero))

    def spread_sum(slots, mine, value, group, sent, received):
        slots[mine] = value
        copies = [
            pltpu.make_async_remote_copy(
                src_ref=slots.at[mine],
                dst_ref=slots.at[mine],
                send_sem=sent.at[i],
                recv_sem=received.at[i],
                device_id=device,
                device_id_type=MESH,
            )
            for i, device in enumerate(group)
        ]
        for copy in copies:
            copy.start()
        for copy in copies:
            copy.wait_recv()
        total = slots[0]
        for i in range(1, len(group) + 1):
            total = total + slots[i]
        return total, copies

    share = jnp.concatenate([dg_q * F32(SCALE), dg_k * F32(1.0 / LOG2E), jnp.zeros((6, HEAD), F32)], axis=0)
    total, copies1 = spread_sum(sum1, seg * shards + me, share, group1, s1_send, s1_recv)
    total, copies2 = spread_sum(sum2, dp, total, group2, s2_send, s2_recv)
    og_ref[...] = total[0:2] * F32(1.0 / (segments * replicas))

    for h in range(heads - together, heads):
        store(h)
    for copy in copies1 + copies2:
        copy.wait_send()

    @pl.loop(0, heads)
    def _(h):
        for copy in outs(h) + parts(h):
            copy.wait_send()
        for copy in stores(h):
            copy.wait()


def hand_over(pieces, *refs):
    ins, outs, holds, sums, in_sem, out_sem = refs[:4], refs[4:8], refs[8:11], refs[11], refs[12], refs[13]
    rows = ins[0].shape[1] // pieces
    todo = []
    for p in range(pieces):
        part = pl.ds(p * rows, rows)
        for i in range(3):
            hold = holds[i].at[part]
            todo.append((
                pltpu.make_async_copy(ins[i].at[0, part], hold, in_sem.at[i, p]),
                pltpu.make_async_copy(hold, outs[i].at[0, part], out_sem.at[i, p]),
            ))
    todo.append((
        pltpu.make_async_copy(ins[3], sums, in_sem.at[3, 0]),
        pltpu.make_async_copy(sums, outs[3], out_sem.at[3, 0]),
    ))
    for load, _ in todo:
        load.start()
    for load, store in todo:
        load.wait()
        store.start()
    for _, store in todo:
        store.wait()


def body(sizes, query_in, key_in, value_in, latent_now, latent_next, gains, rewards, steps, counts):
    segments, replicas, shards = sizes
    _, rows, full = query_in.shape
    length, width = rows * shards, full // shards
    heads = width // HEAD
    any_space = pl.BlockSpec(memory_space=pltpu.HBM)
    vmem = pl.BlockSpec(memory_space=pltpu.VMEM)
    smem = pl.BlockSpec(memory_space=pltpu.SMEM)
    grad = jax.ShapeDtypeStruct((1, length, width), BF16)
    near, far = segments * shards, replicas
    dma = pltpu.SemaphoreType.DMA
    results = pl.pallas_call(
        functools.partial(kernel, sizes),
        out_shape=(grad, grad, grad, jax.ShapeDtypeStruct((2, HEAD), F32)),
        in_specs=[any_space] * 5 + [vmem] + [smem] * 3,
        out_specs=(any_space, any_space, any_space, vmem),
        scratch_shapes=[pltpu.VMEM((rows, full), BF16)] * 3
        + [pltpu.VMEM((heads, length, HEAD), BF16)] * 4
        + [pltpu.VMEM((2, rows, full), BF16), pltpu.VMEM((rows, full), BF16)]
        + [pltpu.VMEM((heads, length, HEAD), BF16)] * 6
        + [pltpu.VMEM((near, 8, HEAD), F32), pltpu.VMEM((far, 8, HEAD), F32)]
        + [dma((5,)), dma((3, heads))]
        + [dma((4, heads, shards - 1))] * 2
        + [dma((3, heads))] * 2
        + [dma((near - 1,))] * 2
        + [dma((far - 1,))] * 2,
        compiler_params=pltpu.CompilerParams(
            collective_id=0, has_side_effects=True, vmem_limit_bytes=63 * 1024 * 1024
        ),
        cost_estimate=pl.CostEstimate(
            flops=12 * heads * length * length * HEAD,
            bytes_accessed=16 * length * width,
            transcendentals=heads * length * length,
        ),
    )(query_in, key_in, value_in, latent_now, latent_next, gains, rewards, steps, counts)
    hbm = pl.BlockSpec(memory_space=pltpu.HBM)
    return pl.pallas_call(
        functools.partial(hand_over, 2),
        out_shape=(grad, grad, grad, jax.ShapeDtypeStruct((2, HEAD), F32)),
        in_specs=[hbm] * 4,
        out_specs=(hbm,) * 4,
        scratch_shapes=[pltpu.VMEM((length, width), BF16)] * 3
        + [pltpu.VMEM((2, HEAD), F32), dma((4, 2)), dma((4, 2))],
        compiler_params=pltpu.CompilerParams(vmem_limit_bytes=63 * 1024 * 1024),
    )(*results)


def solution(mesh):
    sizes = tuple(mesh.shape[name] for name in ("segment", "dp", "seq"))
    rows = P(("segment", "dp"), "seq", None)
    columns = P(("segment", "dp"), None, "seq")
    return jax.shard_map(
        functools.partial(body, sizes),
        mesh=mesh,
        in_specs=(rows,) * 5 + (P(),) * 4,
        out_specs=(columns, columns, columns, P()),
        check_vma=False,
    )
```

```python
import functools

import jax
import jax.numpy as jnp
from jax import lax
from jax.experimental import pallas as pl
from jax.experimental.pallas import tpu as pltpu
from jax.sharding import PartitionSpec as P

HEAD = 128
STEPS = 16
GROUP = 16
AHEAD = 3
LOG2E = 1.4426950408889634
SCALE = HEAD ** -0.5
MESH = pl.DeviceIdType.MESH
F32 = jnp.float32
BF16 = jnp.bfloat16


def dot(a, b, da, db):
    return lax.dot_general(a, b, (((da,), (db,)), ((), ())), preferred_element_type=F32)


def inverse_rms(wide, average):
    return lax.rsqrt(dot((wide * wide).astype(BF16), average, 1, 0) + 1e-06)


def unit_rows_back(grad, unit, r, gain, average):
    inner = grad * gain
    mean = dot((inner * unit).astype(BF16), average, 1, 0)
    return r * (inner - unit * mean), jnp.sum(grad * unit, axis=0, keepdims=True)


def sigma(index):
    level = 1.0 - index.astype(F32) / STEPS
    return 7.0 * level / (1.0 + 6.0 * level)


def kernel(
    sizes,
    q_ref, k_ref, v_ref, now_ref, next_ref, gains_ref, reward_ref, step_ref, count_ref,
    oq_ref, ok_ref, ov_ref, og_ref,
    qs, ks, vs, qb, kb, vb, db, lat, diff, gq, gk, gv, sum1, sum2,
    load_sem, store_sem, send_sem, recv_sem, s1_send, s1_recv, s2_send, s2_recv,
):
    segments, replicas, shards = sizes
    seg, dp, me = (lax.axis_index(name) for name in ("segment", "dp", "seq"))
    rows, heads = q_ref.shape[1], qb.shape[0]
    width = heads * HEAD

    loads = [
        pltpu.make_async_copy(ref.at[0], dst, load_sem.at[i])
        for i, (ref, dst) in enumerate(
            ((q_ref, qs), (k_ref, ks), (v_ref, vs), (now_ref, lat.at[0]), (next_ref, lat.at[1]))
        )
    ]
    for copy in loads:
        copy.start()

    sources = (qs, ks, vs, diff)
    targets = (qb, kb, vb, db)
    my_rows = pl.ds(pl.multiple_of(me * rows, rows), rows)

    group1 = [
        (lax.rem(seg + a, segments), dp, lax.rem(me + b, shards))
        for a in range(segments)
        for b in range(shards)
        if a or b
    ]
    group2 = [(seg, lax.rem(dp + a, replicas), me) for a in range(1, replicas)]
    barrier = pltpu.get_barrier_semaphore()
    for device in group1 + group2:
        pl.semaphore_signal(barrier, inc=1, device_id=device, device_id_type=MESH)
    pl.semaphore_wait(barrier, len(group1) + len(group2))

    def part(array, head, step):
        other = lax.rem(me + step, shards)
        columns = pl.ds(pl.multiple_of(other * width + head * HEAD, HEAD), HEAD)
        return pltpu.make_async_remote_copy(
            src_ref=sources[array].at[:, columns],
            dst_ref=targets[array].at[head, my_rows],
            send_sem=send_sem.at[array, head, step],
            recv_sem=recv_sem.at[array, head, step],
            device_id=(lax.rem(seg + 1, segments), dp, other),
            device_id_type=MESH,
        )

    def parts(head, arrays=(0, 1, 2, 3)):
        return [part(i, head, s) for i in arrays for s in range(shards)]

    def send(head, arrays=(0, 1, 2, 3)):
        for copy in parts(head, arrays):
            copy.start()

    together = next(n for n in (1,) if heads % n == 0)
    groups = heads // together
    ahead = min(AHEAD, groups)

    def send_group(g, arrays=(0, 1, 2, 3)):
        for i in arrays:
            for j in range(together):
                send(g * together + j, (i,))

    for i in range(3):
        loads[i].wait()
        send_group(0, (i,))
    for copy in loads[3:]:
        copy.wait()
    full = diff.shape[1]
    for c in range(0, full, 256):
        cols = slice(c, c + 256)
        diff[:, cols] = (lat[1, :, cols].astype(F32) - lat[0, :, cols].astype(F32)).astype(BF16)
    send_group(0, (3,))
    for g in range(1, ahead):
        send_group(g)

    video = lax.rem(seg + segments - 1, segments) * replicas + dp
    first = video // GROUP * GROUP
    one = (1, 1)
    rewards = [reward_ref[first + i] for i in range(GROUP)]
    mean = sum(rewards[1:], rewards[0]) * F32(1.0 / GROUP)
    spread = sum((r - mean) * (r - mean) for r in rewards) * F32(1.0 / GROUP)
    spread = jnp.sqrt(jnp.full(one, spread, F32))
    advantage = jnp.full(one, reward_ref[video] - mean, F32) / jnp.maximum(spread, F32(0.25))
    step = jnp.full(one, step_ref[video], jnp.int32)
    delta = sigma(step) - sigma(step + 1)
    count = count_ref[video]
    q_gain, k_gain = gains_ref[0:1], gains_ref[1:2]
    q_gain_log2 = q_gain * F32(SCALE * LOG2E)
    dq_gain, dk_gain = q_gain * F32(SCALE), k_gain * F32(1.0 / LOG2E)
    length = qb.shape[1]
    average = jnp.full((HEAD, HEAD), 1.0 / HEAD, BF16)
    ones = jnp.full((length, HEAD), 1.0, BF16)
    valid = lax.broadcasted_iota(jnp.int32, (length, HEAD), 0) < count
    row_scale = jnp.where(valid, advantage, F32(0.0))
    valid_ones = jnp.where(valid, F32(1.0), F32(0.0)).astype(BF16)

    def wide_lanes(x):
        return jnp.concatenate([x] * (length // HEAD), axis=1)

    def stores(head):
        cols = pl.ds(pl.multiple_of(head * HEAD, HEAD), HEAD)
        return [
            pltpu.make_async_copy(src.at[head], dst.at[0, :, cols], store_sem.at[i, head])
            for i, (src, dst) in enumerate(((gq, oq_ref), (gk, ok_ref), (gv, ov_ref)))
        ]

    def wait(hs, array):
        for h in hs:
            for copy in parts(h, (array,)):
                copy.wait_recv()

    def one_group(g, sums):
        hs = [g * together + j for j in range(together)]
        wait(hs, 0)

        @pl.when(g + ahead < groups)
        def _():
            send_group(g + ahead)

        wait(hs, 1)
        q_wide = [qb[h].astype(F32) for h in hs]
        k_wide = [kb[h].astype(F32) for h in hs]
        q_r = [inverse_rms(x, average) for x in q_wide]
        k_r = [jnp.where(valid, inverse_rms(x, average), F32(0.0)) for x in k_wide]
        q_unit = [x * r for x, r in zip(q_wide, q_r)]
        k_unit = [x * r for x, r in zip(k_wide, k_r)]
        q = [(x * q_gain_log2).astype(BF16) for x in q_unit]
        k = [(x * k_gain).astype(BF16) for x in k_unit]
        raw = [jnp.exp2(dot(a, b, 1, 1)) for a, b in zip(q, k)]
        weights = [x.astype(BF16) for x in raw]
        inverse = [1.0 / dot(x, valid_ones, 1, 0) for x in weights]
        raw_by_key = [jnp.exp2(dot(a, b, 1, 1)) for a, b in zip(k, q)]
        weights_by_key = [x.astype(BF16) for x in raw_by_key]
        wait(hs, 2)
        v = [vb[h] * valid_ones for h in hs]
        velocity = [dot(x, y, 1, 0) * z for x, y, z in zip(weights, v, inverse)]
        wait(hs, 3)
        cotangent = [
            (row_scale * z * (db[h].astype(F32) + delta * x)).astype(BF16)
            for h, x, z in zip(hs, velocity, inverse)
        ]
        for h, x, y in zip(hs, weights_by_key, cotangent):
            gv[h] = jnp.where(valid, dot(x, y, 1, 0), F32(0.0)).astype(BF16)
        along = [(x.astype(F32) * y).astype(BF16) for x, y in zip(cotangent, velocity)]
        inner = [dot(x, ones[:HEAD], 1, 0) for x in along]
        inner_by_key = [dot(ones, x, 1, 1) for x in along]
        ds_by_key = [
            (z * (dot(x, y, 1, 1) - i)).astype(BF16)
            for x, y, z, i in zip(v, cotangent, raw_by_key, inner_by_key)
        ]
        ds = [
            (z * (dot(y, x, 1, 1) - wide_lanes(i))).astype(BF16)
            for x, y, z, i in zip(v, cotangent, raw, inner)
        ]
        dk = [
            unit_rows_back(dot(x, y, 1, 0), u, r, dk_gain, average)
            for x, y, u, r in zip(ds_by_key, q, k_unit, k_r)
        ]
        dq = [
            unit_rows_back(dot(x, y, 1, 0), u, r, dq_gain, average)
            for x, y, u, r in zip(ds, k, q_unit, q_r)
        ]
        for h, x, y in zip(hs, dq, dk):
            gq[h], gk[h] = x[0].astype(BF16), y[0].astype(BF16)
        for h in hs:
            for copy in stores(h):
                copy.start()
        return sum((x[1] for x in dq), sums[0]), sum((x[1] for x in dk), sums[1])

    zero = jnp.zeros((1, HEAD), F32)
    dg_q, dg_k = lax.fori_loop(0, groups, one_group, (zero, zero))

    def spread_sum(slots, mine, value, group, sent, received):
        slots[mine] = value
        copies = [
            pltpu.make_async_remote_copy(
                src_ref=slots.at[mine],
                dst_ref=slots.at[mine],
                send_sem=sent.at[i],
                recv_sem=received.at[i],
                device_id=device,
                device_id_type=MESH,
            )
            for i, device in enumerate(group)
        ]
        for copy in copies:
            copy.start()
        for copy in copies:
            copy.wait_recv()
        total = slots[0]
        for i in range(1, len(group) + 1):
            total = total + slots[i]
        return total, copies

    share = jnp.concatenate([dg_q * F32(SCALE), dg_k * F32(1.0 / LOG2E), jnp.zeros((6, HEAD), F32)], axis=0)
    total, copies1 = spread_sum(sum1, seg * shards + me, share, group1, s1_send, s1_recv)
    total, copies2 = spread_sum(sum2, dp, total, group2, s2_send, s2_recv)
    og_ref[...] = total[0:2] * F32(1.0 / (segments * replicas))

    for copy in copies1 + copies2:
        copy.wait_send()

    @pl.loop(0, heads)
    def _(h):
        for copy in parts(h):
            copy.wait_send()
        for copy in stores(h):
            copy.wait()


def hand_over(pieces, *refs):
    ins, outs, holds, sums, in_sem, out_sem = refs[:4], refs[4:8], refs[8:11], refs[11], refs[12], refs[13]
    rows = ins[0].shape[1] // pieces
    todo = []
    for p in range(pieces):
        part = pl.ds(p * rows, rows)
        for i in range(3):
            hold = holds[i].at[part]
            todo.append((
                pltpu.make_async_copy(ins[i].at[0, part], hold, in_sem.at[i, p]),
                pltpu.make_async_copy(hold, outs[i].at[0, part], out_sem.at[i, p]),
            ))
    todo.append((
        pltpu.make_async_copy(ins[3], sums, in_sem.at[3, 0]),
        pltpu.make_async_copy(sums, outs[3], out_sem.at[3, 0]),
    ))
    for load, _ in todo:
        load.start()
    for load, store in todo:
        load.wait()
        store.start()
    for _, store in todo:
        store.wait()


def body(sizes, query_in, key_in, value_in, latent_now, latent_next, gains, rewards, steps, counts):
    segments, replicas, shards = sizes
    _, rows, full = query_in.shape
    length, width = rows * shards, full // shards
    heads = width // HEAD
    any_space = pl.BlockSpec(memory_space=pltpu.HBM)
    vmem = pl.BlockSpec(memory_space=pltpu.VMEM)
    smem = pl.BlockSpec(memory_space=pltpu.SMEM)
    grad = jax.ShapeDtypeStruct((1, length, width), BF16)
    near, far = segments * shards, replicas
    dma = pltpu.SemaphoreType.DMA
    results = pl.pallas_call(
        functools.partial(kernel, sizes),
        out_shape=(grad, grad, grad, jax.ShapeDtypeStruct((2, HEAD), F32)),
        in_specs=[any_space] * 5 + [vmem] + [smem] * 3,
        out_specs=(any_space, any_space, any_space, vmem),
        scratch_shapes=[pltpu.VMEM((rows, full), BF16)] * 3
        + [pltpu.VMEM((heads, length, HEAD), BF16)] * 4
        + [pltpu.VMEM((2, rows, full), BF16), pltpu.VMEM((rows, full), BF16)]
        + [pltpu.VMEM((heads, length, HEAD), BF16)] * 3
        + [pltpu.VMEM((near, 8, HEAD), F32), pltpu.VMEM((far, 8, HEAD), F32)]
        + [dma((5,)), dma((3, heads))]
        + [dma((4, heads, shards))] * 2
        + [dma((near - 1,))] * 2
        + [dma((far - 1,))] * 2,
        compiler_params=pltpu.CompilerParams(
            collective_id=0, has_side_effects=True, vmem_limit_bytes=63 * 1024 * 1024
        ),
        cost_estimate=pl.CostEstimate(
            flops=12 * heads * length * length * HEAD,
            bytes_accessed=16 * length * width,
            transcendentals=heads * length * length,
        ),
    )(query_in, key_in, value_in, latent_now, latent_next, gains, rewards, steps, counts)
    hbm = pl.BlockSpec(memory_space=pltpu.HBM)
    return pl.pallas_call(
        functools.partial(hand_over, 2),
        out_shape=(grad, grad, grad, jax.ShapeDtypeStruct((2, HEAD), F32)),
        in_specs=[hbm] * 4,
        out_specs=(hbm,) * 4,
        scratch_shapes=[pltpu.VMEM((length, width), BF16)] * 3
        + [pltpu.VMEM((2, HEAD), F32), dma((4, 2)), dma((4, 2))],
        compiler_params=pltpu.CompilerParams(vmem_limit_bytes=63 * 1024 * 1024),
    )(*results)


def solution(mesh):
    sizes = tuple(mesh.shape[name] for name in ("segment", "dp", "seq"))
    rows = P(("segment", "dp"), "seq", None)
    columns = P(("segment", "dp"), None, "seq")
    return jax.shard_map(
        functools.partial(body, sizes),
        mesh=mesh,
        in_specs=(rows,) * 5 + (P(),) * 4,
        out_specs=(columns, columns, columns, P()),
        check_vma=False,
    )
```

```python
import functools

import jax
import jax.numpy as jnp
from jax import lax
from jax.experimental import pallas as pl
from jax.experimental.pallas import tpu as pltpu
from jax.sharding import PartitionSpec as P

HEAD = 128
STEPS = 16
GROUP = 16
AHEAD = 3
LOG2E = 1.4426950408889634
SCALE = HEAD ** -0.5
MESH = pl.DeviceIdType.MESH
F32 = jnp.float32
BF16 = jnp.bfloat16


def dot(a, b, da, db):
    return lax.dot_general(a, b, (((da,), (db,)), ((), ())), preferred_element_type=F32)


def inverse_rms(wide, average):
    return lax.rsqrt(dot((wide * wide).astype(BF16), average, 1, 0) + 1e-06)


def unit_rows_back(grad, unit, r, gain, average):
    inner = grad * gain
    mean = dot((inner * unit).astype(BF16), average, 1, 0)
    return r * (inner - unit * mean), jnp.sum(grad * unit, axis=0, keepdims=True)


def sigma(index):
    level = 1.0 - index.astype(F32) / STEPS
    return 7.0 * level / (1.0 + 6.0 * level)


def kernel(
    sizes,
    q_ref, k_ref, v_ref, now_ref, next_ref, gains_ref, reward_ref, step_ref, count_ref,
    oq_ref, ok_ref, ov_ref, og_ref,
    qs, ks, vs, lat, ready, held, gq, gk, gv, sum1, sum2,
    load_sem, store_sem, send_sem, recv_sem, s1_send, s1_recv, s2_send, s2_recv,
):
    segments, replicas, shards = sizes
    seg, dp, me = (lax.axis_index(name) for name in ("segment", "dp", "seq"))
    rows, heads = q_ref.shape[1], held.shape[1]
    width = heads * HEAD

    loads = [
        pltpu.make_async_copy(ref.at[0], dst, load_sem.at[i])
        for i, (ref, dst) in enumerate(
            ((q_ref, qs), (k_ref, ks), (v_ref, vs), (now_ref, lat.at[0]), (next_ref, lat.at[1]))
        )
    ]
    for copy in loads:
        copy.start()

    my_rows = pl.ds(pl.multiple_of(me * rows, rows), rows)

    group1 = [
        (lax.rem(seg + a, segments), dp, lax.rem(me + b, shards))
        for a in range(segments)
        for b in range(shards)
        if a or b
    ]
    group2 = [(seg, lax.rem(dp + a, replicas), me) for a in range(1, replicas)]
    barrier = pltpu.get_barrier_semaphore()
    for device in group1 + group2:
        pl.semaphore_signal(barrier, inc=1, device_id=device, device_id_type=MESH)

    for i, ref in enumerate((qs, ks, vs)):
        loads[i].wait()
        for h in range(heads * shards):
            ready[i // 2, h, i % 2] = ref[:, h * HEAD : (h + 1) * HEAD]
    for copy in loads[3:]:
        copy.wait()
    for h in range(heads * shards):
        cols = slice(h * HEAD, (h + 1) * HEAD)
        change = lat[1, :, cols].astype(F32) - lat[0, :, cols].astype(F32)
        ready[1, h, 1] = change.astype(BF16)
    pl.semaphore_wait(barrier, len(group1) + len(group2))

    def parts(head, pairs=(0, 1)):
        copies = []
        for pair in pairs:
            for step in range(shards):
                other = lax.rem(me + step, shards)
                copies.append(pltpu.make_async_remote_copy(
                    src_ref=ready.at[pair, other * heads + head],
                    dst_ref=held.at[pair, head, :, my_rows],
                    send_sem=send_sem.at[pair, head, step],
                    recv_sem=recv_sem.at[pair, head, step],
                    device_id=(lax.rem(seg + 1, segments), dp, other),
                    device_id_type=MESH,
                ))
        return copies

    def send(head):
        for copy in parts(head):
            copy.start()

    together = 1
    groups = heads // together
    ahead = min(AHEAD, groups)
    for h in range(ahead):
        send(h)

    video = lax.rem(seg + segments - 1, segments) * replicas + dp
    first = video // GROUP * GROUP
    one = (1, 1)
    rewards = [reward_ref[first + i] for i in range(GROUP)]
    mean = sum(rewards[1:], rewards[0]) * F32(1.0 / GROUP)
    spread = sum((r - mean) * (r - mean) for r in rewards) * F32(1.0 / GROUP)
    spread = jnp.sqrt(jnp.full(one, spread, F32))
    advantage = jnp.full(one, reward_ref[video] - mean, F32) / jnp.maximum(spread, F32(0.25))
    step = jnp.full(one, step_ref[video], jnp.int32)
    delta = sigma(step) - sigma(step + 1)
    count = count_ref[video]
    q_gain, k_gain = gains_ref[0:1], gains_ref[1:2]
    q_gain_log2 = q_gain * F32(SCALE * LOG2E)
    dq_gain, dk_gain = q_gain * F32(SCALE), k_gain * F32(1.0 / LOG2E)
    length = held.shape[3]
    average = jnp.full((HEAD, HEAD), 1.0 / HEAD, BF16)
    ones = jnp.full((length, HEAD), 1.0, BF16)
    valid = lax.broadcasted_iota(jnp.int32, (length, HEAD), 0) < count
    row_scale = jnp.where(valid, advantage, F32(0.0))
    valid_ones = jnp.where(valid, F32(1.0), F32(0.0)).astype(BF16)

    def wide_lanes(x):
        return jnp.concatenate([x] * (length // HEAD), axis=1)

    def stores(head):
        cols = pl.ds(pl.multiple_of(head * HEAD, HEAD), HEAD)
        return [
            pltpu.make_async_copy(src.at[head], dst.at[0, :, cols], store_sem.at[i, head])
            for i, (src, dst) in enumerate(((gq, oq_ref), (gk, ok_ref), (gv, ov_ref)))
        ]

    def wait(hs, pair):
        for h in hs:
            for copy in parts(h, (pair,)):
                copy.wait_recv()

    def one_group(g, sums):
        hs = [g * together + j for j in range(together)]
        wait(hs, 0)

        @pl.when(g + ahead < groups)
        def _():
            send(g + ahead)

        q_wide = [held[0, h, 0].astype(F32) for h in hs]
        k_wide = [held[0, h, 1].astype(F32) for h in hs]
        q_r = [inverse_rms(x, average) for x in q_wide]
        k_r = [jnp.where(valid, inverse_rms(x, average), F32(0.0)) for x in k_wide]
        q_unit = [x * r for x, r in zip(q_wide, q_r)]
        k_unit = [x * r for x, r in zip(k_wide, k_r)]
        q = [(x * q_gain_log2).astype(BF16) for x in q_unit]
        k = [(x * k_gain).astype(BF16) for x in k_unit]
        raw = [jnp.exp2(dot(a, b, 1, 1)) for a, b in zip(q, k)]
        weights = [x.astype(BF16) for x in raw]
        inverse = [1.0 / dot(x, valid_ones, 1, 0) for x in weights]
        raw_by_key = [jnp.exp2(dot(a, b, 1, 1)) for a, b in zip(k, q)]
        weights_by_key = [x.astype(BF16) for x in raw_by_key]
        wait(hs, 1)
        v = [held[1, h, 0] * valid_ones for h in hs]
        velocity = [dot(x, y, 1, 0) * z for x, y, z in zip(weights, v, inverse)]
        cotangent = [
            (row_scale * z * (held[1, h, 1].astype(F32) + delta * x)).astype(BF16)
            for h, x, z in zip(hs, velocity, inverse)
        ]
        for h, x, y in zip(hs, weights_by_key, cotangent):
            gv[h] = jnp.where(valid, dot(x, y, 1, 0), F32(0.0)).astype(BF16)
        along = [(x.astype(F32) * y).astype(BF16) for x, y in zip(cotangent, velocity)]
        inner = [dot(x, ones[:HEAD], 1, 0) for x in along]
        inner_by_key = [dot(ones, x, 1, 1) for x in along]
        ds_by_key = [
            (z * (dot(x, y, 1, 1) - i)).astype(BF16)
            for x, y, z, i in zip(v, cotangent, raw_by_key, inner_by_key)
        ]
        ds = [
            (z * (dot(y, x, 1, 1) - wide_lanes(i))).astype(BF16)
            for x, y, z, i in zip(v, cotangent, raw, inner)
        ]
        dk = [
            unit_rows_back(dot(x, y, 1, 0), u, r, dk_gain, average)
            for x, y, u, r in zip(ds_by_key, q, k_unit, k_r)
        ]
        dq = [
            unit_rows_back(dot(x, y, 1, 0), u, r, dq_gain, average)
            for x, y, u, r in zip(ds, k, q_unit, q_r)
        ]
        for h, x, y in zip(hs, dq, dk):
            gq[h], gk[h] = x[0].astype(BF16), y[0].astype(BF16)
        for h in hs:
            for copy in stores(h):
                copy.start()
        return sum((x[1] for x in dq), sums[0]), sum((x[1] for x in dk), sums[1])

    zero = jnp.zeros((1, HEAD), F32)
    dg_q, dg_k = lax.fori_loop(0, groups, one_group, (zero, zero))

    def spread_sum(slots, mine, value, group, sent, received):
        slots[mine] = value
        copies = [
            pltpu.make_async_remote_copy(
                src_ref=slots.at[mine],
                dst_ref=slots.at[mine],
                send_sem=sent.at[i],
                recv_sem=received.at[i],
                device_id=device,
                device_id_type=MESH,
            )
            for i, device in enumerate(group)
        ]
        for copy in copies:
            copy.start()
        for copy in copies:
            copy.wait_recv()
        total = slots[0]
        for i in range(1, len(group) + 1):
            total = total + slots[i]
        return total, copies

    share = jnp.concatenate([dg_q * F32(SCALE), dg_k * F32(1.0 / LOG2E), jnp.zeros((6, HEAD), F32)], axis=0)
    total, copies1 = spread_sum(sum1, seg * shards + me, share, group1, s1_send, s1_recv)
    total, copies2 = spread_sum(sum2, dp, total, group2, s2_send, s2_recv)
    og_ref[...] = total[0:2] * F32(1.0 / (segments * replicas))

    for copy in copies1 + copies2:
        copy.wait_send()

    @pl.loop(0, heads)
    def _(h):
        for copy in parts(h):
            copy.wait_send()
        for copy in stores(h):
            copy.wait()


def hand_over(pieces, *refs):
    ins, outs, holds, sums, in_sem, out_sem = refs[:4], refs[4:8], refs[8:11], refs[11], refs[12], refs[13]
    rows = ins[0].shape[1] // pieces
    todo = []
    for p in range(pieces):
        part = pl.ds(p * rows, rows)
        for i in range(3):
            hold = holds[i].at[part]
            todo.append((
                pltpu.make_async_copy(ins[i].at[0, part], hold, in_sem.at[i, p]),
                pltpu.make_async_copy(hold, outs[i].at[0, part], out_sem.at[i, p]),
            ))
    todo.append((
        pltpu.make_async_copy(ins[3], sums, in_sem.at[3, 0]),
        pltpu.make_async_copy(sums, outs[3], out_sem.at[3, 0]),
    ))
    for load, _ in todo:
        load.start()
    for load, store in todo:
        load.wait()
        store.start()
    for _, store in todo:
        store.wait()


def body(sizes, query_in, key_in, value_in, latent_now, latent_next, gains, rewards, steps, counts):
    segments, replicas, shards = sizes
    _, rows, full = query_in.shape
    length, width = rows * shards, full // shards
    heads = width // HEAD
    any_space = pl.BlockSpec(memory_space=pltpu.HBM)
    vmem = pl.BlockSpec(memory_space=pltpu.VMEM)
    smem = pl.BlockSpec(memory_space=pltpu.SMEM)
    grad = jax.ShapeDtypeStruct((1, length, width), BF16)
    near, far = segments * shards, replicas
    dma = pltpu.SemaphoreType.DMA
    results = pl.pallas_call(
        functools.partial(kernel, sizes),
        out_shape=(grad, grad, grad, jax.ShapeDtypeStruct((2, HEAD), F32)),
        in_specs=[any_space] * 5 + [vmem] + [smem] * 3,
        out_specs=(any_space, any_space, any_space, vmem),
        scratch_shapes=[pltpu.VMEM((rows, full), BF16)] * 3
        + [pltpu.VMEM((2, rows, full), BF16), pltpu.VMEM((2, full // HEAD, 2, rows, HEAD), BF16)]
        + [pltpu.VMEM((2, heads, 2, length, HEAD), BF16)]
        + [pltpu.VMEM((heads, length, HEAD), BF16)] * 3
        + [pltpu.VMEM((near, 8, HEAD), F32), pltpu.VMEM((far, 8, HEAD), F32)]
        + [dma((5,)), dma((3, heads))]
        + [dma((2, heads, shards))] * 2
        + [dma((near - 1,))] * 2
        + [dma((far - 1,))] * 2,
        compiler_params=pltpu.CompilerParams(
            collective_id=0, has_side_effects=True, vmem_limit_bytes=63 * 1024 * 1024
        ),
        cost_estimate=pl.CostEstimate(
            flops=12 * heads * length * length * HEAD,
            bytes_accessed=16 * length * width,
            transcendentals=heads * length * length,
        ),
    )(query_in, key_in, value_in, latent_now, latent_next, gains, rewards, steps, counts)
    hbm = pl.BlockSpec(memory_space=pltpu.HBM)
    return pl.pallas_call(
        functools.partial(hand_over, 2),
        out_shape=(grad, grad, grad, jax.ShapeDtypeStruct((2, HEAD), F32)),
        in_specs=[hbm] * 4,
        out_specs=(hbm,) * 4,
        scratch_shapes=[pltpu.VMEM((length, width), BF16)] * 3
        + [pltpu.VMEM((2, HEAD), F32), dma((4, 2)), dma((4, 2))],
        compiler_params=pltpu.CompilerParams(vmem_limit_bytes=63 * 1024 * 1024),
    )(*results)


def solution(mesh):
    sizes = tuple(mesh.shape[name] for name in ("segment", "dp", "seq"))
    rows = P(("segment", "dp"), "seq", None)
    columns = P(("segment", "dp"), None, "seq")
    return jax.shard_map(
        functools.partial(body, sizes),
        mesh=mesh,
        in_specs=(rows,) * 5 + (P(),) * 4,
        out_specs=(columns, columns, columns, P()),
        check_vma=False,
    )
```

```python
import functools

import jax
import jax.numpy as jnp
from jax import lax
from jax.experimental import pallas as pl
from jax.experimental.pallas import tpu as pltpu
from jax.sharding import PartitionSpec as P

HEAD = 128
STEPS = 16
GROUP = 16
AHEAD = 6
LOG2E = 1.4426950408889634
SCALE = HEAD ** -0.5
MESH = pl.DeviceIdType.MESH
F32 = jnp.float32
BF16 = jnp.bfloat16


def dot(a, b, da, db):
    return lax.dot_general(a, b, (((da,), (db,)), ((), ())), preferred_element_type=F32)


def inverse_rms(wide):
    return lax.rsqrt(jnp.mean(wide * wide, axis=-1, keepdims=True) + 1e-06)


def unit_rows_back(grad, unit, r, gain):
    inner = grad * gain
    mean = jnp.mean(inner * unit, axis=-1, keepdims=True)
    return r * (inner - unit * mean), jnp.sum(grad * unit, axis=0, keepdims=True)


def sigma(index):
    level = 1.0 - index.astype(F32) / STEPS
    return 7.0 * level / (1.0 + 6.0 * level)


def kernel(
    sizes,
    q_ref, k_ref, v_ref, now_ref, next_ref, gains_ref, reward_ref, step_ref, count_ref,
    oq_ref, ok_ref, ov_ref, og_ref,
    qs, ks, vs, lat, ready, held, gq, gk, gv, sum1, sum2,
    load_sem, store_sem, send_sem, recv_sem, s1_send, s1_recv, s2_send, s2_recv,
):
    segments, replicas, shards = sizes
    seg, dp, me = (lax.axis_index(name) for name in ("segment", "dp", "seq"))
    rows, heads = q_ref.shape[1], held.shape[1]
    width = heads * HEAD

    loads = [
        pltpu.make_async_copy(ref.at[0], dst, load_sem.at[i])
        for i, (ref, dst) in enumerate(
            ((q_ref, qs), (k_ref, ks), (v_ref, vs), (now_ref, lat.at[0]), (next_ref, lat.at[1]))
        )
    ]
    for copy in loads:
        copy.start()

    my_rows = pl.ds(pl.multiple_of(me * rows, rows), rows)

    group1 = [
        (lax.rem(seg + a, segments), dp, lax.rem(me + b, shards))
        for a in range(segments)
        for b in range(shards)
        if a or b
    ]
    group2 = [(seg, lax.rem(dp + a, replicas), me) for a in range(1, replicas)]
    barrier = pltpu.get_barrier_semaphore()
    for device in group1 + group2:
        pl.semaphore_signal(barrier, inc=1, device_id=device, device_id_type=MESH)

    for i, ref in enumerate((qs, ks, vs)):
        loads[i].wait()
        for h in range(heads * shards):
            ready[i // 2, h, i % 2] = ref[:, h * HEAD : (h + 1) * HEAD]
    for copy in loads[3:]:
        copy.wait()
    for h in range(heads * shards):
        cols = slice(h * HEAD, (h + 1) * HEAD)
        change = lat[1, :, cols].astype(F32) - lat[0, :, cols].astype(F32)
        ready[1, h, 1] = change.astype(BF16)
    pl.semaphore_wait(barrier, len(group1) + len(group2))

    def parts(head, pairs=(0, 1)):
        copies = []
        for pair in pairs:
            for step in range(shards):
                other = lax.rem(me + step, shards)
                copies.append(pltpu.make_async_remote_copy(
                    src_ref=ready.at[pair, other * heads + head],
                    dst_ref=held.at[pair, head, :, my_rows],
                    send_sem=send_sem.at[pair, head, step],
                    recv_sem=recv_sem.at[pair, head, step],
                    device_id=(lax.rem(seg + 1, segments), dp, other),
                    device_id_type=MESH,
                ))
        return copies

    def send(head):
        for copy in parts(head):
            copy.start()

    together = 1
    groups = heads // together
    ahead = min(AHEAD, groups)
    for h in range(ahead):
        send(h)

    video = lax.rem(seg + segments - 1, segments) * replicas + dp
    first = video // GROUP * GROUP
    one = (1, 1)
    rewards = [reward_ref[first + i] for i in range(GROUP)]
    mean = sum(rewards[1:], rewards[0]) * F32(1.0 / GROUP)
    spread = sum((r - mean) * (r - mean) for r in rewards) * F32(1.0 / GROUP)
    spread = jnp.sqrt(jnp.full(one, spread, F32))
    advantage = jnp.full(one, reward_ref[video] - mean, F32) / jnp.maximum(spread, F32(0.25))
    step = jnp.full(one, step_ref[video], jnp.int32)
    delta = sigma(step) - sigma(step + 1)
    count = count_ref[video]
    q_gain, k_gain = gains_ref[0:1], gains_ref[1:2]
    q_gain_log2 = q_gain * F32(SCALE * LOG2E)
    dq_gain, dk_gain = q_gain * F32(SCALE), k_gain * F32(1.0 / LOG2E)
    length = held.shape[3]
    valid = lax.broadcasted_iota(jnp.int32, (length, HEAD), 0) < count
    valid_column = lax.broadcasted_iota(jnp.int32, (length, 1), 0) < count
    row_scale = jnp.where(valid, advantage, F32(0.0))
    valid_ones = jnp.where(valid, F32(1.0), F32(0.0)).astype(BF16)
    minus_ones = jnp.full((length, HEAD), -1.0, BF16)

    def beside(x, y):
        return jnp.concatenate([x, y], axis=1)

    def stores(head):
        cols = pl.ds(pl.multiple_of(head * HEAD, HEAD), HEAD)
        return [
            pltpu.make_async_copy(src.at[head], dst.at[0, :, cols], store_sem.at[i, head])
            for i, (src, dst) in enumerate(((gq, oq_ref), (gk, ok_ref), (gv, ov_ref)))
        ]

    def wait(hs, pair):
        for h in hs:
            for copy in parts(h, (pair,)):
                copy.wait_recv()

    def one_group(g, sums):
        hs = [g * together + j for j in range(together)]
        wait(hs, 0)

        @pl.when(g + ahead < groups)
        def _():
            send(g + ahead)

        q_wide = [held[0, h, 0].astype(F32) for h in hs]
        k_wide = [held[0, h, 1].astype(F32) for h in hs]
        q_r = [inverse_rms(x) for x in q_wide]
        k_r = [jnp.where(valid_column, inverse_rms(x), F32(0.0)) for x in k_wide]
        q_unit = [x * r for x, r in zip(q_wide, q_r)]
        k_unit = [x * r for x, r in zip(k_wide, k_r)]
        q = [(x * q_gain_log2).astype(BF16) for x in q_unit]
        k = [(x * k_gain).astype(BF16) for x in k_unit]
        raw = [jnp.exp2(dot(a, b, 1, 1)) for a, b in zip(q, k)]
        weights = [x.astype(BF16) for x in raw]
        raw_by_key = [jnp.exp2(dot(a, b, 1, 1)) for a, b in zip(k, q)]
        weights_by_key = [x.astype(BF16) for x in raw_by_key]
        wait(hs, 1)
        v = [held[1, h, 0] * valid_ones for h in hs]
        summed = [dot(x, beside(y, valid_ones), 1, 0) for x, y in zip(weights, v)]
        inverse = [1.0 / x[:, HEAD:] for x in summed]
        velocity = [x[:, :HEAD] * y for x, y in zip(summed, inverse)]
        cotangent = [
            (row_scale * z * (held[1, h, 1].astype(F32) + delta * x)).astype(BF16)
            for h, x, z in zip(hs, velocity, inverse)
        ]
        for h, x, y in zip(hs, weights_by_key, cotangent):
            gv[h] = jnp.where(valid, dot(x, y, 1, 0), F32(0.0)).astype(BF16)
        left = [
            beside(x, (x.astype(F32) * y).astype(BF16)) for x, y in zip(cotangent, velocity)
        ]
        right = [beside(x, minus_ones) for x in v]
        ds = [(z * dot(x, y, 1, 1)).astype(BF16) for x, y, z in zip(left, right, raw)]
        ds_by_key = [
            (z * dot(y, x, 1, 1)).astype(BF16) for x, y, z in zip(left, right, raw_by_key)
        ]
        dq = [
            unit_rows_back(dot(x, y, 1, 0), u, r, dq_gain)
            for x, y, u, r in zip(ds, k, q_unit, q_r)
        ]
        dk = [
            unit_rows_back(dot(x, y, 1, 0), u, r, dk_gain)
            for x, y, u, r in zip(ds_by_key, q, k_unit, k_r)
        ]
        for h, x, y in zip(hs, dq, dk):
            gq[h], gk[h] = x[0].astype(BF16), y[0].astype(BF16)
        for h in hs:
            for copy in stores(h):
                copy.start()
        return sum((x[1] for x in dq), sums[0]), sum((x[1] for x in dk), sums[1])

    zero = jnp.zeros((1, HEAD), F32)
    dg_q, dg_k = lax.fori_loop(0, groups, one_group, (zero, zero))

    def spread_sum(slots, mine, value, group, sent, received):
        slots[mine] = value
        copies = [
            pltpu.make_async_remote_copy(
                src_ref=slots.at[mine],
                dst_ref=slots.at[mine],
                send_sem=sent.at[i],
                recv_sem=received.at[i],
                device_id=device,
                device_id_type=MESH,
            )
            for i, device in enumerate(group)
        ]
        for copy in copies:
            copy.start()
        for copy in copies:
            copy.wait_recv()
        total = slots[0]
        for i in range(1, len(group) + 1):
            total = total + slots[i]
        return total, copies

    share = jnp.concatenate([dg_q * F32(SCALE), dg_k * F32(1.0 / LOG2E), jnp.zeros((6, HEAD), F32)], axis=0)
    total, copies1 = spread_sum(sum1, seg * shards + me, share, group1, s1_send, s1_recv)
    total, copies2 = spread_sum(sum2, dp, total, group2, s2_send, s2_recv)
    og_ref[...] = total[0:2] * F32(1.0 / (segments * replicas))

    for copy in copies1 + copies2:
        copy.wait_send()

    @pl.loop(0, heads)
    def _(h):
        for copy in parts(h):
            copy.wait_send()
        for copy in stores(h):
            copy.wait()


def hand_over(pieces, *refs):
    ins, outs, holds, sums, in_sem, out_sem = refs[:4], refs[4:8], refs[8:11], refs[11], refs[12], refs[13]
    rows = ins[0].shape[1] // pieces
    todo = []
    for p in range(pieces):
        part = pl.ds(p * rows, rows)
        for i in range(3):
            hold = holds[i].at[part]
            todo.append((
                pltpu.make_async_copy(ins[i].at[0, part], hold, in_sem.at[i, p]),
                pltpu.make_async_copy(hold, outs[i].at[0, part], out_sem.at[i, p]),
            ))
    todo.append((
        pltpu.make_async_copy(ins[3], sums, in_sem.at[3, 0]),
        pltpu.make_async_copy(sums, outs[3], out_sem.at[3, 0]),
    ))
    for load, _ in todo:
        load.start()
    for load, store in todo:
        load.wait()
        store.start()
    for _, store in todo:
        store.wait()


def body(sizes, query_in, key_in, value_in, latent_now, latent_next, gains, rewards, steps, counts):
    segments, replicas, shards = sizes
    _, rows, full = query_in.shape
    length, width = rows * shards, full // shards
    heads = width // HEAD
    any_space = pl.BlockSpec(memory_space=pltpu.HBM)
    vmem = pl.BlockSpec(memory_space=pltpu.VMEM)
    smem = pl.BlockSpec(memory_space=pltpu.SMEM)
    grad = jax.ShapeDtypeStruct((1, length, width), BF16)
    near, far = segments * shards, replicas
    dma = pltpu.SemaphoreType.DMA
    results = pl.pallas_call(
        functools.partial(kernel, sizes),
        out_shape=(grad, grad, grad, jax.ShapeDtypeStruct((2, HEAD), F32)),
        in_specs=[any_space] * 5 + [vmem] + [smem] * 3,
        out_specs=(any_space, any_space, any_space, vmem),
        scratch_shapes=[pltpu.VMEM((rows, full), BF16)] * 3
        + [pltpu.VMEM((2, rows, full), BF16), pltpu.VMEM((2, full // HEAD, 2, rows, HEAD), BF16)]
        + [pltpu.VMEM((2, heads, 2, length, HEAD), BF16)]
        + [pltpu.VMEM((heads, length, HEAD), BF16)] * 3
        + [pltpu.VMEM((near, 8, HEAD), F32), pltpu.VMEM((far, 8, HEAD), F32)]
        + [dma((5,)), dma((3, heads))]
        + [dma((2, heads, shards))] * 2
        + [dma((near - 1,))] * 2
        + [dma((far - 1,))] * 2,
        compiler_params=pltpu.CompilerParams(
            collective_id=0, has_side_effects=True, vmem_limit_bytes=63 * 1024 * 1024
        ),
        cost_estimate=pl.CostEstimate(
            flops=12 * heads * length * length * HEAD,
            bytes_accessed=16 * length * width,
            transcendentals=heads * length * length,
        ),
    )(query_in, key_in, value_in, latent_now, latent_next, gains, rewards, steps, counts)
    hbm = pl.BlockSpec(memory_space=pltpu.HBM)
    return pl.pallas_call(
        functools.partial(hand_over, 2),
        out_shape=(grad, grad, grad, jax.ShapeDtypeStruct((2, HEAD), F32)),
        in_specs=[hbm] * 4,
        out_specs=(hbm,) * 4,
        scratch_shapes=[pltpu.VMEM((length, width), BF16)] * 3
        + [pltpu.VMEM((2, HEAD), F32), dma((4, 2)), dma((4, 2))],
        compiler_params=pltpu.CompilerParams(vmem_limit_bytes=63 * 1024 * 1024),
    )(*results)


def solution(mesh):
    sizes = tuple(mesh.shape[name] for name in ("segment", "dp", "seq"))
    rows = P(("segment", "dp"), "seq", None)
    columns = P(("segment", "dp"), None, "seq")
    return jax.shard_map(
        functools.partial(body, sizes),
        mesh=mesh,
        in_specs=(rows,) * 5 + (P(),) * 4,
        out_specs=(columns, columns, columns, P()),
        check_vma=False,
    )
```

```python
import functools

import jax
import jax.numpy as jnp
from jax import lax
from jax.experimental import pallas as pl
from jax.experimental.pallas import tpu as pltpu
from jax.sharding import PartitionSpec as P

HEAD = 128
STEPS = 16
GROUP = 16
AHEAD = 6
LOG2E = 1.4426950408889634
SCALE = HEAD ** -0.5
MESH = pl.DeviceIdType.MESH
F32 = jnp.float32
BF16 = jnp.bfloat16


def dot(a, b, da, db):
    return lax.dot_general(a, b, (((da,), (db,)), ((), ())), preferred_element_type=F32)


def inverse_rms(wide):
    return lax.rsqrt(jnp.mean(wide * wide, axis=-1, keepdims=True) + 1e-06)


def unit_rows_back(grad, unit, r, gain):
    inner = grad * gain
    mean = jnp.mean(inner * unit, axis=-1, keepdims=True)
    return r * (inner - unit * mean), jnp.sum(grad * unit, axis=0, keepdims=True)


def sigma(index):
    level = 1.0 - index.astype(F32) / STEPS
    return 7.0 * level / (1.0 + 6.0 * level)


def kernel(
    sizes,
    q_ref, k_ref, v_ref, now_ref, next_ref, gains_ref, reward_ref, step_ref, count_ref,
    oq_ref, ok_ref, ov_ref, og_ref,
    qs, ks, vs, lat, ready, held, gq, gk, gv, sum1, sum2,
    load_sem, store_sem, send_sem, recv_sem, s1_send, s1_recv, s2_send, s2_recv,
):
    segments, replicas, shards = sizes
    seg, dp, me = (lax.axis_index(name) for name in ("segment", "dp", "seq"))
    rows, heads = q_ref.shape[1], held.shape[1]
    width = heads * HEAD

    loads = [
        pltpu.make_async_copy(ref.at[0], dst, load_sem.at[i])
        for i, (ref, dst) in enumerate(
            ((q_ref, qs), (k_ref, ks), (v_ref, vs), (now_ref, lat.at[0]), (next_ref, lat.at[1]))
        )
    ]
    for copy in loads:
        copy.start()

    my_rows = pl.ds(pl.multiple_of(me * rows, rows), rows)

    group1 = [
        (lax.rem(seg + a, segments), dp, lax.rem(me + b, shards))
        for a in range(segments)
        for b in range(shards)
        if a or b
    ]
    group2 = [(seg, lax.rem(dp + a, replicas), me) for a in range(1, replicas)]
    barrier = pltpu.get_barrier_semaphore()
    for device in group1 + group2:
        pl.semaphore_signal(barrier, inc=1, device_id=device, device_id_type=MESH)

    for i, ref in enumerate((qs, ks, vs)):
        loads[i].wait()
        for h in range(heads * shards):
            ready[i // 2, h, i % 2] = ref[:, h * HEAD : (h + 1) * HEAD]
    for copy in loads[3:]:
        copy.wait()
    for h in range(heads * shards):
        cols = slice(h * HEAD, (h + 1) * HEAD)
        change = lat[1, :, cols].astype(F32) - lat[0, :, cols].astype(F32)
        ready[1, h, 1] = change.astype(BF16)
    pl.semaphore_wait(barrier, len(group1) + len(group2))

    def parts(head, pairs=(0, 1)):
        copies = []
        for pair in pairs:
            for step in reversed(range(shards)):
                other = lax.rem(me + step, shards)
                copies.append(pltpu.make_async_remote_copy(
                    src_ref=ready.at[pair, other * heads + head],
                    dst_ref=held.at[pair, head, :, my_rows],
                    send_sem=send_sem.at[pair, head, step],
                    recv_sem=recv_sem.at[pair, head, step],
                    device_id=(lax.rem(seg + 1, segments), dp, other),
                    device_id_type=MESH,
                ))
        return copies

    def send(head):
        for copy in parts(head):
            copy.start()

    together = 1
    groups = heads // together
    ahead = min(AHEAD, groups)
    for h in range(ahead):
        send(h)

    video = lax.rem(seg + segments - 1, segments) * replicas + dp
    first = video // GROUP * GROUP
    one = (1, 1)
    rewards = [reward_ref[first + i] for i in range(GROUP)]
    mean = sum(rewards[1:], rewards[0]) * F32(1.0 / GROUP)
    spread = sum((r - mean) * (r - mean) for r in rewards) * F32(1.0 / GROUP)
    spread = jnp.sqrt(jnp.full(one, spread, F32))
    advantage = jnp.full(one, reward_ref[video] - mean, F32) / jnp.maximum(spread, F32(0.25))
    step = jnp.full(one, step_ref[video], jnp.int32)
    delta = sigma(step) - sigma(step + 1)
    count = count_ref[video]
    q_gain, k_gain = gains_ref[0:1], gains_ref[1:2]
    q_gain_log2 = q_gain * F32(SCALE * LOG2E)
    dq_gain, dk_gain = q_gain * F32(SCALE), k_gain * F32(1.0 / LOG2E)
    length = held.shape[3]
    valid = lax.broadcasted_iota(jnp.int32, (length, HEAD), 0) < count
    valid_column = lax.broadcasted_iota(jnp.int32, (length, 1), 0) < count
    row_scale = jnp.where(valid, advantage, F32(0.0))
    valid_ones = jnp.where(valid, F32(1.0), F32(0.0)).astype(BF16)
    minus_ones = jnp.full((length, HEAD), -1.0, BF16)

    def beside(x, y):
        return jnp.concatenate([x, y], axis=1)

    def stores(head):
        cols = pl.ds(pl.multiple_of(head * HEAD, HEAD), HEAD)
        return [
            pltpu.make_async_copy(src.at[head], dst.at[0, :, cols], store_sem.at[i, head])
            for i, (src, dst) in enumerate(((gq, oq_ref), (gk, ok_ref), (gv, ov_ref)))
        ]

    def wait(hs, pair):
        for h in hs:
            for copy in parts(h, (pair,)):
                copy.wait_recv()

    def one_group(g, sums):
        hs = [g * together + j for j in range(together)]
        wait(hs, 0)

        @pl.when(g + ahead < groups)
        def _():
            send(g + ahead)

        q_wide = [held[0, h, 0].astype(F32) for h in hs]
        k_wide = [held[0, h, 1].astype(F32) for h in hs]
        q_r = [inverse_rms(x) for x in q_wide]
        k_r = [jnp.where(valid_column, inverse_rms(x), F32(0.0)) for x in k_wide]
        q_unit = [x * r for x, r in zip(q_wide, q_r)]
        k_unit = [x * r for x, r in zip(k_wide, k_r)]
        q = [(x * q_gain_log2).astype(BF16) for x in q_unit]
        k = [(x * k_gain).astype(BF16) for x in k_unit]
        raw = [jnp.exp2(dot(a, b, 1, 1)) for a, b in zip(q, k)]
        weights = [x.astype(BF16) for x in raw]
        raw_by_key = [jnp.exp2(dot(a, b, 1, 1)) for a, b in zip(k, q)]
        weights_by_key = [x.astype(BF16) for x in raw_by_key]
        wait(hs, 1)
        v = [held[1, h, 0] * valid_ones for h in hs]
        summed = [dot(x, beside(y, valid_ones), 1, 0) for x, y in zip(weights, v)]
        inverse = [1.0 / x[:, HEAD:] for x in summed]
        velocity = [x[:, :HEAD] * y for x, y in zip(summed, inverse)]
        cotangent = [
            (row_scale * z * (held[1, h, 1].astype(F32) + delta * x)).astype(BF16)
            for h, x, z in zip(hs, velocity, inverse)
        ]
        for h, x, y in zip(hs, weights_by_key, cotangent):
            gv[h] = jnp.where(valid, dot(x, y, 1, 0), F32(0.0)).astype(BF16)
        left = [
            beside(x, (x.astype(F32) * y).astype(BF16)) for x, y in zip(cotangent, velocity)
        ]
        right = [beside(x, minus_ones) for x in v]
        ds = [(z * dot(x, y, 1, 1)).astype(BF16) for x, y, z in zip(left, right, raw)]
        ds_by_key = [
            (z * dot(y, x, 1, 1)).astype(BF16) for x, y, z in zip(left, right, raw_by_key)
        ]
        dq = [
            unit_rows_back(dot(x, y, 1, 0), u, r, dq_gain)
            for x, y, u, r in zip(ds, k, q_unit, q_r)
        ]
        dk = [
            unit_rows_back(dot(x, y, 1, 0), u, r, dk_gain)
            for x, y, u, r in zip(ds_by_key, q, k_unit, k_r)
        ]
        for h, x, y in zip(hs, dq, dk):
            gq[h], gk[h] = x[0].astype(BF16), y[0].astype(BF16)
        for h in hs:
            for copy in stores(h):
                copy.start()
        return sum((x[1] for x in dq), sums[0]), sum((x[1] for x in dk), sums[1])

    zero = jnp.zeros((1, HEAD), F32)
    dg_q, dg_k = lax.fori_loop(0, groups, one_group, (zero, zero))

    def spread_sum(slots, mine, value, group, sent, received):
        slots[mine] = value
        copies = [
            pltpu.make_async_remote_copy(
                src_ref=slots.at[mine],
                dst_ref=slots.at[mine],
                send_sem=sent.at[i],
                recv_sem=received.at[i],
                device_id=device,
                device_id_type=MESH,
            )
            for i, device in enumerate(group)
        ]
        for copy in copies:
            copy.start()
        for copy in copies:
            copy.wait_recv()
        total = slots[0]
        for i in range(1, len(group) + 1):
            total = total + slots[i]
        return total, copies

    share = jnp.concatenate([dg_q * F32(SCALE), dg_k * F32(1.0 / LOG2E), jnp.zeros((6, HEAD), F32)], axis=0)
    total, copies1 = spread_sum(sum1, seg * shards + me, share, group1, s1_send, s1_recv)
    total, copies2 = spread_sum(sum2, dp, total, group2, s2_send, s2_recv)
    og_ref[...] = total[0:2] * F32(1.0 / (segments * replicas))

    for copy in copies1 + copies2:
        copy.wait_send()

    @pl.loop(0, heads)
    def _(h):
        for copy in parts(h):
            copy.wait_send()
        for copy in stores(h):
            copy.wait()


def hand_over(pieces, *refs):
    ins, outs, holds, sums, in_sem, out_sem = refs[:4], refs[4:8], refs[8:11], refs[11], refs[12], refs[13]
    rows = ins[0].shape[1] // pieces
    todo = []
    for p in range(pieces):
        part = pl.ds(p * rows, rows)
        for i in range(3):
            hold = holds[i].at[part]
            todo.append((
                pltpu.make_async_copy(ins[i].at[0, part], hold, in_sem.at[i, p]),
                pltpu.make_async_copy(hold, outs[i].at[0, part], out_sem.at[i, p]),
            ))
    todo.append((
        pltpu.make_async_copy(ins[3], sums, in_sem.at[3, 0]),
        pltpu.make_async_copy(sums, outs[3], out_sem.at[3, 0]),
    ))
    for load, _ in todo:
        load.start()
    for load, store in todo:
        load.wait()
        store.start()
    for _, store in todo:
        store.wait()


def body(sizes, query_in, key_in, value_in, latent_now, latent_next, gains, rewards, steps, counts):
    segments, replicas, shards = sizes
    _, rows, full = query_in.shape
    length, width = rows * shards, full // shards
    heads = width // HEAD
    any_space = pl.BlockSpec(memory_space=pltpu.HBM)
    vmem = pl.BlockSpec(memory_space=pltpu.VMEM)
    smem = pl.BlockSpec(memory_space=pltpu.SMEM)
    grad = jax.ShapeDtypeStruct((1, length, width), BF16)
    near, far = segments * shards, replicas
    dma = pltpu.SemaphoreType.DMA
    results = pl.pallas_call(
        functools.partial(kernel, sizes),
        out_shape=(grad, grad, grad, jax.ShapeDtypeStruct((2, HEAD), F32)),
        in_specs=[any_space] * 5 + [vmem] + [smem] * 3,
        out_specs=(any_space, any_space, any_space, vmem),
        scratch_shapes=[pltpu.VMEM((rows, full), BF16)] * 3
        + [pltpu.VMEM((2, rows, full), BF16), pltpu.VMEM((2, full // HEAD, 2, rows, HEAD), BF16)]
        + [pltpu.VMEM((2, heads, 2, length, HEAD), BF16)]
        + [pltpu.VMEM((heads, length, HEAD), BF16)] * 3
        + [pltpu.VMEM((near, 8, HEAD), F32), pltpu.VMEM((far, 8, HEAD), F32)]
        + [dma((5,)), dma((3, heads))]
        + [dma((2, heads, shards))] * 2
        + [dma((near - 1,))] * 2
        + [dma((far - 1,))] * 2,
        compiler_params=pltpu.CompilerParams(
            collective_id=0, has_side_effects=True, vmem_limit_bytes=63 * 1024 * 1024
        ),
        cost_estimate=pl.CostEstimate(
            flops=12 * heads * length * length * HEAD,
            bytes_accessed=16 * length * width,
            transcendentals=heads * length * length,
        ),
    )(query_in, key_in, value_in, latent_now, latent_next, gains, rewards, steps, counts)
    hbm = pl.BlockSpec(memory_space=pltpu.HBM)
    return pl.pallas_call(
        functools.partial(hand_over, 4),
        out_shape=(grad, grad, grad, jax.ShapeDtypeStruct((2, HEAD), F32)),
        in_specs=[hbm] * 4,
        out_specs=(hbm,) * 4,
        scratch_shapes=[pltpu.VMEM((length, width), BF16)] * 3
        + [pltpu.VMEM((2, HEAD), F32), dma((4, 4)), dma((4, 4))],
        compiler_params=pltpu.CompilerParams(vmem_limit_bytes=63 * 1024 * 1024),
    )(*results)


def solution(mesh):
    sizes = tuple(mesh.shape[name] for name in ("segment", "dp", "seq"))
    rows = P(("segment", "dp"), "seq", None)
    columns = P(("segment", "dp"), None, "seq")
    return jax.shard_map(
        functools.partial(body, sizes),
        mesh=mesh,
        in_specs=(rows,) * 5 + (P(),) * 4,
        out_specs=(columns, columns, columns, P()),
        check_vma=False,
    )
```
